32 devices in a mesh: wide: 8 (over z, y), narrow: 4 (over x, core).
Axes of the slice: x: 2, y: 2, z: 4, core: 2. Of those that a mesh axis runs over, the one named last changes fastest.
Arguments:
- raw_ints: bfloat16 [4, 640, 8, 2, 384], P('narrow', 'wide'), may hold values from -5 to 5
- metric_root: bfloat16 [640, 640], P('wide'), may hold values from -0.25 to 0.25
- occ_energy: float32 [8, 2], replicated, may hold values from -1.6 to -0.4
- vir_energy: float32 [4, 384], replicated, may hold values from 0.3 to 2.5
- block_kpoint: int32 [4, 8], replicated, may hold values from 0 to 7
- occ_count: int32 [4, 8], replicated, may hold values from 1 to 2, as said below
Outputs:
- gamma: bfloat16 [4, 640, 8, 2, 384], P('narrow', None, 'wide')
- virt_density: float32 [147456], P(('wide', 'narrow'))
The draws below stay inside these ranges and needn't reach their ends.
Inputs may be any that keep to these rules, and one draw needn't show every extreme that they name: `occ_count`: slot o of a block is live when o is less than its count; some block has all 2 slots live.
All inputs are finite; a program needn't handle non-finite values.
Results may differ from the reference program's by a relative error of at most 0.0043.
Values may be sent and summed in bfloat16 or wider, within the bound.
No kernel may reach another device: no remote copies, remote signals or barrier semaphores. Data moves between devices by JAX's collectives and lax.ppermute only.
A program may use at most 64 MiB of HBM per device.

```python
import jax
import jax.numpy as jnp
from jax import lax

NAUX = 640
V = 384
OCC = 2
WINDOW = 3
NKPT = 8
BLOCKS = 8
KGROUPS = 4


def draw_occ_count(key, part):
    first_key = jax.random.fold_in(key, 11)
    second_key = jax.random.fold_in(key, 23)
    counts = jax.random.randint(first_key, (KGROUPS * BLOCKS,), 1, OCC + 1)
    chosen = jax.random.randint(second_key, (), 0, KGROUPS * BLOCKS)
    counts = counts.at[chosen].set(OCC)
    return counts.reshape(KGROUPS, BLOCKS).astype(jnp.int32)


def draw_raw_ints(key, part):
    noise_key = jax.random.fold_in(key, 101)
    sign_key = jax.random.fold_in(key, 103)
    profile_key = jax.random.fold_in(key, 107)
    phase_key = jax.random.fold_in(key, 109)
    pairing_key = jax.random.fold_in(key, 113)
    full_shape = (KGROUPS, NAUX, BLOCKS, OCC, V)
    noise = jnp.clip(0.15 * jax.random.normal(noise_key, full_shape, jnp.float32), -0.9, 0.9)
    profiles = jnp.clip(jax.random.normal(profile_key, (2, V), jnp.float32), -3.0, 3.0)
    slice_rows = NAUX // BLOCKS
    pairing = jax.random.permutation(pairing_key, BLOCKS)
    slice_index = jnp.arange(NAUX, dtype=jnp.int32) // slice_rows
    spiked = pairing[slice_index][:, None] == jnp.arange(BLOCKS, dtype=jnp.int32)[None, :]
    boost = jnp.where(spiked, 5.0, 1.0).astype(jnp.float32)
    signs = jax.random.randint(sign_key, (KGROUPS, NAUX, BLOCKS, OCC), 0, 2).astype(jnp.float32) * 2.0 - 1.0
    phase = jax.random.randint(phase_key, (), 0, 8).astype(jnp.float32) * (jnp.pi / 4.0)
    angle = phase + jnp.pi / 4.0 * jnp.arange(BLOCKS, dtype=jnp.float32)
    profile = jnp.cos(angle)[:, None] * profiles[0][None, :] + jnp.sin(angle)[:, None] * profiles[1][None, :]
    values = noise * boost[None, :, :, None, None] + 0.2 * signs[..., None] * profile[None, None, :, None, :]
    return jnp.clip(values, -5.0, 5.0).astype(jnp.bfloat16)


def plant(array, stream_key, least, top_value):
    longest = array.shape.index(max(array.shape))
    spots = []
    for shift in (0, 1):
        where = [jax.random.randint(jax.random.fold_in(stream_key, axis), (), 0, length) for axis, length in enumerate(array.shape)]
        where[longest] = (where[longest] + shift) % array.shape[longest]
        spots.append(tuple(where))
    return array.at[spots[0]].set(least).at[spots[1]].set(top_value)


def shard_levels(key, shape, shards, least, largest):
    def one(dim, parts):
        steps = jax.random.uniform(jax.random.fold_in(jax.random.fold_in(key, 6), dim), (parts,), jnp.float32, least / len(shards), largest / len(shards))
        return jnp.repeat(jnp.exp(steps), shape[dim] // parts).reshape((-1,) + (1,) * (len(shape) - dim - 1))

    level = one(*shards[0])
    for cut in shards[1:]:
        level = level * one(*cut)
    return level


def centred(own_key, dims, scale, bound, split=(), kind=jnp.bfloat16):
    drawn = jax.random.normal(own_key, dims, jnp.float32) * scale
    if len(split) > 0:
        drawn = shard_levels(own_key, dims, split, -0.22, 0.18) * drawn
    return jnp.clip(drawn, min=-bound, max=bound).astype(kind)


def setup_inputs(seed: int = 0) -> dict:
    splits = jax.random.split(jax.random.key(seed), 7)
    raw_ints = draw_raw_ints(jax.random.fold_in(splits[6], 71), 0)
    metric_root = centred(splits[1], (NAUX, NAUX), NAUX ** -0.5, 0.25, ((0, 8),))
    occ_energy = jnp.clip(jax.random.uniform(splits[2], (NKPT, OCC), jnp.float32, -1.6, -0.4), -1.6, -0.4)
    vir_energy = jnp.clip(jax.random.uniform(splits[3], (KGROUPS, V), jnp.float32, 0.3, 2.5), 0.3, 2.5)
    block_kpoint = plant(jax.random.randint(splits[4], (KGROUPS, BLOCKS), 0, NKPT), jax.random.fold_in(splits[4], 1), 0, NKPT - 1).astype(jnp.int32)
    occ_count = draw_occ_count(jax.random.fold_in(splits[6], 71), 0)
    return {"raw_ints": raw_ints, "metric_root": metric_root, "occ_energy": occ_energy, "vir_energy": vir_energy, "block_kpoint": block_kpoint, "occ_count": occ_count}


def reference(raw_ints, metric_root, occ_energy, vir_energy, block_kpoint, occ_count):
    group_count, aux_count, block_count, occ_slots, vir_count = raw_ints.shape
    row_width = occ_slots * vir_count
    stacked = []
    for group_id in range(group_count):
        aux_rows = raw_ints[group_id].reshape(aux_count, block_count * row_width)
        product = lax.dot_general(metric_root, aux_rows, (((0,), (0,)), ((), ())), preferred_element_type=jnp.float32)
        stacked.append(product.astype(jnp.bfloat16).reshape(aux_count, block_count, row_width))
    fitted = jnp.stack(stacked)
    occ_block = occ_energy[block_kpoint]
    live = (jnp.arange(occ_slots, dtype=jnp.int32)[None, None, :] < occ_count[:, :, None]).astype(jnp.float32)
    norm_scale = 1.0 / (group_count * block_count * vir_count)

    def one_block(density, position):
        group_id = position // block_count
        my_block = position % block_count
        partner_group = (group_id + group_count // 2) % group_count
        own_rows = fitted[group_id, :, my_block]
        vir_own = vir_energy[group_id]
        vir_partner = vir_energy[partner_group]
        occ_own = occ_block[group_id, my_block]
        live_own = live[group_id, my_block]
        gamma_sum = jnp.zeros((aux_count, row_width), jnp.float32)
        for offset in range(WINDOW):
            other_block = (my_block + offset) % block_count
            far_rows = fitted[partner_group, :, other_block]
            coulomb = lax.dot_general(own_rows, far_rows, (((0,), (0,)), ((), ())), preferred_element_type=jnp.float32)
            coulomb = coulomb.reshape(occ_slots, vir_count, occ_slots, vir_count)
            denominator = (occ_own[:, None, None, None] + occ_block[partner_group, other_block][None, None, :, None]
                           - vir_own[None, :, None, None] - vir_partner[None, None, None, :])
            amplitude = coulomb / denominator * live_own[:, None, None, None] * live[partner_group, other_block][None, None, :, None]
            mixed_amp = 2.0 * amplitude - jnp.transpose(amplitude, (0, 3, 2, 1))
            amp_half = amplitude.astype(jnp.bfloat16)
            mixed_half = mixed_amp.astype(jnp.bfloat16)
            gamma_sum = gamma_sum + lax.dot_general(far_rows, mixed_half.reshape(row_width, row_width), (((1,), (1,)), ((), ())), preferred_element_type=jnp.float32)
            density = density + jnp.einsum('iajc,ibjc->ab', mixed_half.astype(jnp.float32), amp_half.astype(jnp.float32))
        return density, gamma_sum.astype(jnp.bfloat16)

    density, gammas = lax.scan(one_block, jnp.zeros((vir_count, vir_count), jnp.float32), jnp.arange(group_count * block_count, dtype=jnp.int32))
    gamma = gammas.reshape(group_count, block_count, aux_count, occ_slots, vir_count).transpose(0, 2, 1, 3, 4)
    return gamma, (density * norm_scale).reshape(-1)
```

```python
import functools

import jax
import jax.numpy as jnp
from jax import lax
from jax.experimental import pallas as pl
from jax.experimental.pallas import tpu as pltpu
from jax.sharding import PartitionSpec as P

WINDOW = 3
DIRECT = 8


def flip(value, axis, mask):
    pairs = [(source, source ^ mask) for source in range(lax.axis_size(axis))]
    return lax.ppermute(value, axis, pairs)


def from_ahead(value, axis, steps):
    count = lax.axis_size(axis)
    pairs = [(source, (source - steps) % count) for source in range(count)]
    return lax.ppermute(value, axis, pairs)


def is_power(count):
    return count & (count - 1) == 0


def bits_of(count):
    return [1 << bit for bit in reversed(range(count.bit_length() - 1))]


def doubled(count):
    order = [0]
    for mask in bits_of(count):
        order = order + [place ^ mask for place in order]
    return order


def pair_kernel(
    offset, slot, occ_ref, kpoint_ref, count_ref, row_ref, column_ref, own_ref, far_ref, *rest
):
    density_in, mixed_ref, density_ref = rest if len(rest) == 3 else (None, *rest)
    group_count, wide_count = kpoint_ref.shape
    occ_slots = occ_ref.shape[1]
    vir_count = row_ref.shape[1]
    group = lax.axis_index("narrow")
    block = lax.axis_index("wide")
    partner = lax.rem(group + group_count // 2, group_count)
    other = lax.rem(block + offset, wide_count)
    spot = lax.broadcasted_iota(jnp.int32, column_ref.shape, 1)
    vir_own = jnp.sum(jnp.where(spot == group, column_ref[...], 0.0), axis=1, keepdims=True)
    vir_far = row_ref[pl.ds(partner, 1), :]
    occ_far = occ_ref[kpoint_ref[partner, other], slot]
    live_far = slot < count_ref[partner, other]
    far = far_ref[...]
    total = None
    for i in range(occ_slots):
        columns = slice(i * vir_count, (i + 1) * vir_count)
        coulomb = lax.dot_general(
            own_ref[:, columns], far, (((0,), (0,)), ((), ())), preferred_element_type=jnp.float32
        )
        occ = occ_ref[kpoint_ref[group, block], i] + occ_far
        live = jnp.logical_and(i < count_ref[group, block], live_far)
        scale = jnp.where(live, 1.0, 0.0).astype(jnp.float32)
        amplitude = coulomb * (scale / ((occ - vir_own) - vir_far))
        mixed = (2.0 * amplitude - amplitude.T).astype(jnp.bfloat16)
        mixed_ref[columns, :] = mixed
        term = lax.dot_general(
            mixed,
            amplitude.astype(jnp.bfloat16),
            (((1,), (1,)), ((), ())),
            preferred_element_type=jnp.float32,
        )
        total = term if total is None else total + term
    density_ref[...] = total if density_in is None else density_in[...] + total


def gamma_kernel(far_count, *refs):
    fars, mixeds, out_ref = refs[:far_count], refs[far_count:-1], refs[-1]
    vir_count = fars[0].shape[1]
    for i in range(out_ref.shape[1] // vir_count):
        columns = slice(i * vir_count, (i + 1) * vir_count)
        total = None
        for far, mixed in zip(fars, mixeds):
            term = lax.dot_general(
                far[...], mixed[columns, :], (((1,), (1,)), ((), ())), preferred_element_type=jnp.float32
            )
            total = term if total is None else total + term
        out_ref[:, columns] = total.astype(out_ref.dtype)


VMEM = pl.BlockSpec(memory_space=pltpu.VMEM)
SMEM = pl.BlockSpec(memory_space=pltpu.SMEM)


def pair_terms(offset, slot, small, own, far, density):
    vir_count = far.shape[1]
    width = own.shape[1]
    operands = [*small, own, far] + ([] if density is None else [density])
    specs = [SMEM] * 3 + [VMEM] * (len(operands) - 3)
    flops = 2 * own.shape[0] * width * vir_count + 2 * width * vir_count * vir_count
    moved = 2 * (own.size + far.size + width * vir_count) + 8 * vir_count * vir_count
    return pl.pallas_call(
        functools.partial(pair_kernel, offset, slot),
        out_shape=(
            jax.ShapeDtypeStruct((width, vir_count), jnp.bfloat16),
            jax.ShapeDtypeStruct((vir_count, vir_count), jnp.float32),
        ),
        in_specs=specs,
        out_specs=(VMEM, VMEM),
        compiler_params=pltpu.CompilerParams(vmem_limit_bytes=32 * 1024 * 1024),
        cost_estimate=pl.CostEstimate(flops=flops, bytes_accessed=moved, transcendentals=0),
    )(*operands)


def three_index(fars, mixeds):
    aux_count = fars[0].shape[0]
    width = mixeds[0].shape[0]
    flops = sum(2 * far.size * width for far in fars)
    moved = 2 * (sum(far.size for far in fars) + sum(mixed.size for mixed in mixeds) + aux_count * width)
    return pl.pallas_call(
        functools.partial(gamma_kernel, len(fars)),
        out_shape=jax.ShapeDtypeStruct((aux_count, width), jnp.bfloat16),
        in_specs=[VMEM] * (len(fars) + len(mixeds)),
        out_specs=VMEM,
        compiler_params=pltpu.CompilerParams(vmem_limit_bytes=48 * 1024 * 1024),
        cost_estimate=pl.CostEstimate(flops=flops, bytes_accessed=moved, transcendentals=0),
    )(*fars, *mixeds)


def gathered_metric(metric):
    wide_count = lax.axis_size("wide")
    columns = metric.shape[1]
    half = columns // 2
    low_bit = lax.axis_index("narrow") % 2
    part = lax.dynamic_slice_in_dim(metric, low_bit * half, half, 1)
    for mask in bits_of(wide_count):
        part = jnp.concatenate([part, flip(part, "wide", mask)], axis=0)
    other = flip(part, "narrow", 1)
    first = jnp.where(low_bit == 0, part, other)
    second = jnp.where(low_bit == 0, other, part)
    return jnp.concatenate([first, second], axis=1)


def scattered_sum(density):
    wide_count = lax.axis_size("wide")
    group_count = lax.axis_size("narrow")
    wide_bits, narrow_bits = bits_of(wide_count), bits_of(group_count)
    part = density.size // (wide_count * group_count)
    lane = 128 if part % 128 == 0 else part
    value = density.reshape([2] * (len(wide_bits) + len(narrow_bits)) + [part // lane, lane])
    stages = [("narrow", mask, len(wide_bits) + place) for place, mask in enumerate(narrow_bits)]
    stages = stages[::-1] + [("wide", mask, place) for place, mask in reversed(list(enumerate(wide_bits)))]
    for axis, mask, dim in stages:
        bit = (lax.axis_index(axis) // mask) % 2
        sent = lax.dynamic_index_in_dim(value, 1 - bit, dim, keepdims=False).astype(jnp.bfloat16)
        kept = lax.dynamic_index_in_dim(value, bit, dim, keepdims=False)
        value = kept + flip(sent, axis, mask).astype(jnp.float32)
    return value.reshape(-1)


def shards(raw_ints, metric_root, occ_energy, vir_energy, block_kpoint, occ_count):
    _, aux_rows, block_count, occ_slots, vir_count = raw_ints.shape
    row_width = occ_slots * vir_count
    wide_count = lax.axis_size("wide")
    group_count = lax.axis_size("narrow")
    my_block = lax.axis_index("wide")
    direct = wide_count <= DIRECT and is_power(wide_count)
    small = (occ_energy, block_kpoint, occ_count, vir_energy, vir_energy.T)
    if direct:
        metric = gathered_metric(metric_root)
    else:
        metric = lax.all_gather(metric_root, "wide", axis=0, tiled=True)

    fitted = []
    for slot in range(occ_slots):
        blocks = jnp.transpose(raw_ints[0, :, :, slot, :], (1, 0, 2))
        if direct:
            pieces = []
            for place in doubled(wide_count):
                piece = lax.dynamic_index_in_dim(blocks, my_block ^ place, 0, keepdims=False)
                pieces.append(flip(piece, "wide", place) if place else piece)
            rows = jnp.concatenate(pieces, axis=0)
        else:
            rows = lax.all_to_all(blocks, "wide", split_axis=0, concat_axis=0, tiled=True)
            rows = rows.reshape(wide_count * aux_rows, vir_count)
        fitted.append(
            lax.dot_general(
                metric, rows, (((0,), (0,)), ((), ())), preferred_element_type=jnp.float32
            ).astype(jnp.bfloat16)
        )
    own = jnp.concatenate(fitted, axis=1)
    aux_count = own.shape[0]

    half_turn = [(source, (source + group_count // 2) % group_count) for source in range(group_count)]
    facing = [lax.ppermute(part, "narrow", half_turn) for part in fitted]
    odd = my_block % 2 == 1
    window = {}
    for slot in range(occ_slots):
        window[0, slot] = facing[slot]
        second = from_ahead(facing[slot], "wide", 2)
        window[2, slot] = second
        if wide_count % 2 == 0:
            window[1, slot] = flip(jnp.where(odd, facing[slot], second), "wide", 1)
        else:
            window[1, slot] = from_ahead(facing[slot], "wide", 1)

    fars, mixeds = [], []
    density = None
    for offset in (0, 2, 1):
        for slot in range(occ_slots):
            far = window[offset, slot]
            mixed, density = pair_terms(offset, slot, small, own, far, density)
            fars.append(far)
            mixeds.append(mixed)
    gamma = three_index(fars, mixeds)
    norm_scale = 1.0 / (group_count * wide_count * vir_count)
    virt_density = scattered_sum(density * norm_scale)
    return gamma.reshape(1, aux_count, 1, occ_slots, vir_count), virt_density


def solution(mesh):
    placed = (P("narrow", "wide", None, None, None), P("wide", None), P(), P(), P(), P())
    return jax.shard_map(
        shards,
        mesh=mesh,
        in_specs=placed,
        out_specs=(P("narrow", None, "wide", None, None), P(("wide", "narrow"))),
        check_vma=False,
    )
```

```python
import functools

import jax
import jax.numpy as jnp
from jax import lax
from jax.experimental import pallas as pl
from jax.experimental.pallas import tpu as pltpu
from jax.sharding import PartitionSpec as P

WINDOW = 3
DIRECT = 8


def flip(value, axis, mask):
    pairs = [(source, source ^ mask) for source in range(lax.axis_size(axis))]
    return lax.ppermute(value, axis, pairs)


def from_ahead(value, axis, steps):
    count = lax.axis_size(axis)
    pairs = [(source, (source - steps) % count) for source in range(count)]
    return lax.ppermute(value, axis, pairs)


def is_power(count):
    return count & (count - 1) == 0


def bits_of(count):
    return [1 << bit for bit in reversed(range(count.bit_length() - 1))]


def doubled(count):
    order = [0]
    for mask in bits_of(count):
        order = order + [place ^ mask for place in order]
    return order


def rows_of(refs):
    return refs[0][...] if len(refs) == 1 else jnp.concatenate([ref[...] for ref in refs], axis=0)


def product(left, right, dims):
    return lax.dot_general(left, right, ((dims[0], dims[1]), ((), ())), preferred_element_type=jnp.float32)


def fit_kernel(halves, own_count, *refs):
    metric_refs, refs = refs[:halves], refs[halves:]
    own_refs, facing_refs, outs = refs[:own_count], refs[own_count:-2], refs[-2:]
    low_bit = lax.axis_index("narrow") % 2
    for sources, out_ref in zip((own_refs, facing_refs), outs):
        rows = rows_of(sources)
        for place, metric_ref in enumerate(metric_refs):
            part = product(metric_ref[...], rows, ((0,), (0,))).astype(out_ref.dtype)
            if halves == 1:
                out_ref[...] = part
            else:
                start = (low_bit if place == 0 else 1 - low_bit) * part.shape[0]
                out_ref[pl.ds(pl.multiple_of(start, part.shape[0]), part.shape[0]), :] = part


def fit(metric, own, facing):
    aux_count = sum(part.shape[1] for part in metric)
    shape = jax.ShapeDtypeStruct((aux_count, own[0].shape[1]), own[0].dtype)
    flops = 4 * aux_count * aux_count * own[0].shape[1]
    moved = 2 * (aux_count * aux_count + 4 * aux_count * own[0].shape[1])
    operands = [*metric, *own, *facing]
    return pl.pallas_call(
        functools.partial(fit_kernel, len(metric), len(own)),
        out_shape=(shape, shape),
        in_specs=[VMEM] * len(operands),
        out_specs=(VMEM, VMEM),
        compiler_params=pltpu.CompilerParams(vmem_limit_bytes=32 * 1024 * 1024),
        cost_estimate=pl.CostEstimate(flops=flops, bytes_accessed=moved, transcendentals=0),
    )(*operands)


def far_rows(refs):
    if len(refs) == 1:
        return refs[0][...]
    odd = lax.axis_index("wide") % 2 == 1
    return jnp.where(odd, refs[0][...], refs[1][...])


def pair_kernel(offset, slot, fars, sums, last, scale_by, *refs):
    occ_ref, kpoint_ref, count_ref, row_ref, column_ref = refs[:5]
    occ_slots = occ_ref.shape[1]
    own_refs, refs = refs[5 : 5 + occ_slots], refs[5 + occ_slots :]
    far_refs, refs = refs[:fars], refs[fars:]
    sum_refs, outs = refs[:sums], refs[sums:]
    group_count, wide_count = kpoint_ref.shape
    vir_count = row_ref.shape[1]
    group = lax.axis_index("narrow")
    block = lax.axis_index("wide")
    partner = lax.rem(group + group_count // 2, group_count)
    other = lax.rem(block + offset, wide_count)
    spot = lax.broadcasted_iota(jnp.int32, column_ref.shape, 1)
    vir_own = jnp.sum(jnp.where(spot == group, column_ref[...], 0.0), axis=1, keepdims=True)
    vir_far = row_ref[pl.ds(partner, 1), :]
    occ_far = occ_ref[kpoint_ref[partner, other], slot]
    live_far = slot < count_ref[partner, other]
    far = far_rows(far_refs)
    total = None
    for i in range(occ_slots):
        columns = slice(i * vir_count, (i + 1) * vir_count)
        coulomb = product(own_refs[i][...], far, ((0,), (0,)))
        occ = occ_ref[kpoint_ref[group, block], i] + occ_far
        live = jnp.logical_and(i < count_ref[group, block], live_far)
        scale = jnp.where(live, 1.0, 0.0).astype(jnp.float32)
        amplitude = coulomb * (scale / ((occ - vir_own) - vir_far))
        mixed = (2.0 * amplitude - amplitude.T).astype(jnp.bfloat16)
        if last:
            outs[-1][columns, :] = mixed
        else:
            three = product(far, mixed, ((1,), (1,)))
            outs[-1][:, columns] = three if not sums else sum_refs[1][:, columns] + three
        term = product(mixed, amplitude.astype(jnp.bfloat16), ((1,), (1,)))
        total = term if total is None else total + term
    if sums:
        total = sum_refs[0][...] + total
    if not last:
        outs[0][...] = total
        return
    total = total * scale_by
    if len(outs) == 2:
        outs[0][...] = total
        return
    sent_ref, kept_ref = outs[:2]
    part = vir_count // (wide_count * group_count)
    order = halving_order(wide_count, group_count)
    total = jnp.concatenate([total[part * place : part * (place + 1)] for place in order], axis=0)
    half = vir_count // 2
    low = group % 2 == 0
    sent_ref[...] = jnp.where(low, total[half:], total[:half]).astype(jnp.bfloat16)
    kept_ref[...] = jnp.where(low, total[:half], total[half:])


def gamma_kernel(sum_ref, mixed_ref, *refs):
    far = far_rows(refs[:-1])
    refs[-1][...] = (sum_ref[...] + product(far, mixed_ref[...], ((1,), (1,)))).astype(refs[-1].dtype)


VMEM = pl.BlockSpec(memory_space=pltpu.VMEM)
SMEM = pl.BlockSpec(memory_space=pltpu.SMEM)


def pair_terms(offset, slot, small, own, far, sums, last=False, scale_by=1.0):
    aux_count, vir_count = far[0].shape
    width = len(own) * vir_count
    density = jax.ShapeDtypeStruct((vir_count, vir_count), jnp.float32)
    gamma = jax.ShapeDtypeStruct((aux_count, width), jnp.float32)
    mixed = jax.ShapeDtypeStruct((width, vir_count), jnp.bfloat16)
    halves = [jax.ShapeDtypeStruct((vir_count // 2, vir_count), kind) for kind in (jnp.bfloat16, jnp.float32)]
    split = vir_count % (lax.axis_size("wide") * lax.axis_size("narrow")) == 0
    shapes = ((*halves, mixed) if split else (density, mixed)) if last else (density, gamma)
    sums = sums[:1] if last else sums
    operands = [*small, *own, *far, *sums]
    flops = 4 * aux_count * width * vir_count + 2 * width * vir_count * vir_count
    moved = 2 * aux_count * (width + vir_count) + 8 * vir_count * vir_count + 8 * aux_count * width
    return pl.pallas_call(
        functools.partial(pair_kernel, offset, slot, len(far), len(sums), last, scale_by),
        out_shape=shapes,
        in_specs=[SMEM] * 3 + [VMEM] * (len(operands) - 3),
        out_specs=tuple([VMEM] * len(shapes)),
        compiler_params=pltpu.CompilerParams(vmem_limit_bytes=32 * 1024 * 1024),
        cost_estimate=pl.CostEstimate(flops=flops, bytes_accessed=moved, transcendentals=0),
    )(*operands)


def three_index(gamma, mixed, far):
    aux_count, width = gamma.shape
    vir_count = mixed.shape[1]
    return pl.pallas_call(
        gamma_kernel,
        out_shape=jax.ShapeDtypeStruct((aux_count, width), jnp.bfloat16),
        in_specs=[VMEM] * (2 + len(far)),
        out_specs=VMEM,
        compiler_params=pltpu.CompilerParams(vmem_limit_bytes=32 * 1024 * 1024),
        cost_estimate=pl.CostEstimate(
            flops=2 * aux_count * width * vir_count, bytes_accessed=6 * gamma.size, transcendentals=0
        ),
    )(gamma, mixed, *far)


def halving_stages(wide_count, group_count):
    stages = [("narrow", mask) for mask in reversed(bits_of(group_count))]
    return stages + [("wide", mask) for mask in reversed(bits_of(wide_count))]


def halving_order(wide_count, group_count):
    order = [0]
    for axis, mask in reversed(halving_stages(wide_count, group_count)):
        step = mask * group_count if axis == "wide" else mask
        order = order + [place + step for place in order]
    return order


def halved_sum(sent, kept, beside):
    stages = halving_stages(lax.axis_size("wide"), lax.axis_size("narrow"))
    for position, (axis, mask) in enumerate(stages):
        value = kept + flip(sent, axis, mask).astype(jnp.float32)
        if position + 1 < len(stages):
            axis, mask = stages[position + 1]
            bit = (lax.axis_index(axis) // mask) % 2
            half = value.shape[0] // 2
            sent = lax.dynamic_slice_in_dim(value, (1 - bit) * half, half, 0).astype(jnp.bfloat16)
            kept = lax.dynamic_slice_in_dim(value, bit * half, half, 0)
            sent = after(sent, beside) if position == 1 else sent
    return value.reshape(-1)


def pack_kernel(slot, raw_ref, *outs):
    block = lax.axis_index("wide")
    for place, out_ref in zip(doubled(raw_ref.shape[1]), outs):
        for part in range(2):
            out_ref[part] = raw_ref[:, jnp.bitwise_xor(block, place ^ part), slot, :]


def packed(raw, slot):
    rows, block_count, _, vir_count = raw.shape
    shape = jax.ShapeDtypeStruct((2, rows, vir_count), raw.dtype)
    count = block_count // 2
    return pl.pallas_call(
        functools.partial(pack_kernel, slot),
        out_shape=tuple([shape] * count),
        in_specs=[VMEM],
        out_specs=tuple([VMEM] * count),
        compiler_params=pltpu.CompilerParams(vmem_limit_bytes=32 * 1024 * 1024),
        cost_estimate=pl.CostEstimate(flops=0, bytes_accessed=6 * raw.size, transcendentals=0),
    )(raw)


def after(value, *earlier):
    return lax.optimization_barrier((value, *earlier))[0]


def gathered_rows(raw, metric):
    wide_count, group_count = lax.axis_size("wide"), lax.axis_size("narrow")
    half_turn = [(source, (source + group_count // 2) % group_count) for source in range(group_count)]
    occ_slots = raw.shape[2]
    half = metric.shape[1] // 2
    places = doubled(wide_count)[: wide_count // 2]
    stages = bits_of(wide_count)
    part = lax.dynamic_slice_in_dim(metric, lax.axis_index("narrow") % 2 * half, half, 1)
    steps = []
    for mask in stages:
        steps.append(flip(part, "wide", mask))
        part = jnp.concatenate([part, steps[-1]], axis=0)
    own, facing = [], []
    for slot in range(occ_slots):
        source = after(raw, steps[0], *earliest) if slot else raw
        messages = packed(source, slot)
        arrived = [flip(message, "wide", place) for message, place in zip(messages[1:], places[1:])]
        earliest = arrived[-1:]
        arrived = [messages[0], *arrived]
        mine, theirs = [jnp.concatenate([message[part] for message in arrived], axis=0) for part in range(2)]
        if slot:
            mine = after(mine, facing[-1][0])
        else:
            theirs = after(theirs, steps[-2])
        first = lax.ppermute(mine, "narrow", half_turn)
        received = flip(theirs, "wide", 1)
        if slot == 0:
            sent = after(received, first, steps[-1])
        else:
            sent = after(received, first)
        own.append([mine, received])
        facing.append([first, lax.ppermute(sent, "narrow", half_turn)])
    return own, facing, [part, flip(part, "narrow", 1)]


def scattered_sum(density):
    wide_count = lax.axis_size("wide")
    group_count = lax.axis_size("narrow")
    wide_bits, narrow_bits = bits_of(wide_count), bits_of(group_count)
    part = density.size // (wide_count * group_count)
    lane = 128 if part % 128 == 0 else part
    value = density.reshape([2] * (len(wide_bits) + len(narrow_bits)) + [part // lane, lane])
    stages = [("narrow", mask, len(wide_bits) + place) for place, mask in enumerate(narrow_bits)]
    stages = stages[::-1] + [("wide", mask, place) for place, mask in reversed(list(enumerate(wide_bits)))]
    for axis, mask, dim in stages:
        bit = (lax.axis_index(axis) // mask) % 2
        sent = lax.dynamic_index_in_dim(value, 1 - bit, dim, keepdims=False).astype(jnp.bfloat16)
        kept = lax.dynamic_index_in_dim(value, bit, dim, keepdims=False)
        value = kept + flip(sent, axis, mask).astype(jnp.float32)
    return value.reshape(-1)


def shards(raw_ints, metric_root, occ_energy, vir_energy, block_kpoint, occ_count):
    _, aux_rows, block_count, occ_slots, vir_count = raw_ints.shape
    wide_count = lax.axis_size("wide")
    group_count = lax.axis_size("narrow")
    my_block = lax.axis_index("wide")
    direct = wide_count <= DIRECT and is_power(wide_count) and wide_count > 2 and group_count % 2 == 0
    small = (occ_energy, block_kpoint, occ_count, vir_energy, vir_energy.T)
    half_turn = [(source, (source + group_count // 2) % group_count) for source in range(group_count)]
    to_even = [(source, source - 1) for source in range(1, wide_count, 2)]
    to_odd = [(source, source + 1) for source in range(0, wide_count, 2)]

    own_rows, facing_rows = [], []
    if direct:
        own_rows, facing_rows, metric = gathered_rows(raw_ints[0], metric_root)
    else:
        metric = [lax.all_gather(metric_root, "wide", axis=0, tiled=True)]
        for slot in range(occ_slots):
            blocks = jnp.transpose(raw_ints[0, :, :, slot, :], (1, 0, 2))
            rows = lax.all_to_all(blocks, "wide", split_axis=0, concat_axis=0, tiled=True)
            rows = rows.reshape(wide_count * aux_rows, vir_count)
            own_rows.append([rows])
            facing_rows.append([lax.ppermute(rows, "narrow", half_turn)])

    own, facing = zip(*[fit(metric, *rows) for rows in zip(own_rows, facing_rows)])
    aux_count = own[0].shape[0]
    pair = functools.partial(pair_terms, small=small, own=own)
    second, first = [], []
    sums = ()
    for slot in range(occ_slots):
        source = after(facing[slot], *sums) if slot else facing[slot]
        second.append(from_ahead(source, "wide", 2))
        if wide_count % 2 == 0:
            first.append([lax.ppermute(facing[slot], "wide", to_even)])
        else:
            first.append([from_ahead(facing[slot], "wide", 1)])
        sums = pair(0, slot, far=[facing[slot]], sums=sums)
    for slot in range(occ_slots):
        if wide_count % 2 == 0:
            source = after(second[slot], *sums)
            first[slot].insert(0, lax.ppermute(source, "wide", to_odd))
        sums = pair(2, slot, far=[second[slot]], sums=sums)
    for slot in range(occ_slots - 1):
        sums = pair(1, slot, far=first[slot], sums=sums)
    norm_scale = 1.0 / (group_count * wide_count * vir_count)
    *terms, mixed = pair(1, occ_slots - 1, far=first[-1], sums=sums, last=True, scale_by=norm_scale)
    gamma = three_index(sums[1], mixed, first[-1])
    if len(terms) == 2:
        virt_density = halved_sum(*terms, gamma)
    else:
        virt_density = scattered_sum(*terms)
    return gamma.reshape(1, aux_count, 1, occ_slots, vir_count), virt_density


def solution(mesh):
    placed = (P("narrow", "wide", None, None, None), P("wide", None), P(), P(), P(), P())
    return jax.shard_map(
        shards,
        mesh=mesh,
        in_specs=placed,
        out_specs=(P("narrow", None, "wide", None, None), P(("wide", "narrow"))),
        check_vma=False,
    )
```

```python
import functools

import jax
import jax.numpy as jnp
from jax import lax
from jax.experimental import pallas as pl
from jax.experimental.pallas import tpu as pltpu
from jax.sharding import PartitionSpec as P

WINDOW = 3
DIRECT = 8
FAR_PARTS = 1


def flip(value, axis, mask):
    pairs = [(source, source ^ mask) for source in range(lax.axis_size(axis))]
    return lax.ppermute(value, axis, pairs)


def from_ahead(value, axis, steps):
    count = lax.axis_size(axis)
    pairs = [(source, (source - steps) % count) for source in range(count)]
    return lax.ppermute(value, axis, pairs)


def is_power(count):
    return count & (count - 1) == 0


def bits_of(count):
    return [1 << bit for bit in reversed(range(count.bit_length() - 1))]


def doubled(count):
    order = [0]
    for mask in bits_of(count):
        order = order + [place ^ mask for place in order]
    return order


def rows_of(refs):
    return refs[0][...] if len(refs) == 1 else jnp.concatenate([ref[...] for ref in refs], axis=0)


def product(left, right, dims):
    return lax.dot_general(left, right, ((dims[0], dims[1]), ((), ())), preferred_element_type=jnp.float32)


def fit_kernel(halves, parts, cuts, *refs):
    metric_refs, refs = refs[:halves], refs[halves:]
    sources, outs = refs[: parts * len(cuts)], refs[parts * len(cuts) :]
    low = lax.axis_index("narrow") % 2 == 0
    for source, cut in enumerate(cuts):
        rows = rows_of(sources[source * parts : (source + 1) * parts])
        fitted = [product(metric_ref[...], rows, ((0,), (0,))) for metric_ref in metric_refs]
        if halves == 2:
            fitted = [jnp.where(low, fitted[0], fitted[1]), jnp.where(low, fitted[1], fitted[0])]
        fitted = jnp.concatenate([part.astype(outs[0].dtype) for part in fitted], axis=0)
        size = fitted.shape[0] // cut
        for place, out_ref in enumerate(outs[:cut]):
            out_ref[...] = fitted[place * size : (place + 1) * size]
        outs = outs[cut:]


def fit(metric, sources, cuts):
    aux_count = sum(half.shape[1] for half in metric)
    vir_count = sources[0][0].shape[1]
    shapes = [
        jax.ShapeDtypeStruct((aux_count // cut, vir_count), sources[0][0].dtype) for cut in cuts for _ in range(cut)
    ]
    operands = [*metric, *[part for source in sources for part in source]]
    flops = 2 * len(sources) * aux_count * aux_count * vir_count
    moved = 2 * aux_count * (aux_count + 2 * len(sources) * vir_count)
    results = pl.pallas_call(
        functools.partial(fit_kernel, len(metric), len(sources[0]), cuts),
        out_shape=tuple(shapes),
        in_specs=[VMEM] * len(operands),
        out_specs=tuple([VMEM] * len(shapes)),
        compiler_params=pltpu.CompilerParams(vmem_limit_bytes=32 * 1024 * 1024),
        cost_estimate=pl.CostEstimate(flops=flops, bytes_accessed=moved, transcendentals=0),
    )(*operands)
    return [list(results[sum(cuts[:place]) : sum(cuts[: place + 1])]) for place in range(len(cuts))]


def choice_kernel(odd_ref, even_ref, out_ref):
    odd = lax.axis_index("wide") % 2 == 1

    @pl.when(odd)
    def _():
        out_ref[...] = odd_ref[...]

    @pl.when(jnp.logical_not(odd))
    def _():
        out_ref[...] = even_ref[...]


def choice(odd, even):
    return pl.pallas_call(
        choice_kernel,
        out_shape=jax.ShapeDtypeStruct(odd.shape, odd.dtype),
        in_specs=[VMEM] * 2,
        out_specs=VMEM,
        compiler_params=pltpu.CompilerParams(vmem_limit_bytes=32 * 1024 * 1024),
        cost_estimate=pl.CostEstimate(flops=0, bytes_accessed=6 * odd.size, transcendentals=0),
    )(odd, even)


def pair_kernel(offset, slot, fars, sums, last, scale_by, *refs):
    occ_ref, kpoint_ref, count_ref, row_ref, column_ref = refs[:5]
    occ_slots = occ_ref.shape[1]
    own_refs, refs = refs[5 : 5 + occ_slots], refs[5 + occ_slots :]
    far_refs, refs = refs[:fars], refs[fars:]
    sum_refs, outs = refs[:sums], refs[sums:]
    group_count, wide_count = kpoint_ref.shape
    vir_count = row_ref.shape[1]
    group = lax.axis_index("narrow")
    block = lax.axis_index("wide")
    partner = lax.rem(group + group_count // 2, group_count)
    other = lax.rem(block + offset, wide_count)
    spot = lax.broadcasted_iota(jnp.int32, column_ref.shape, 1)
    vir_own = jnp.sum(jnp.where(spot == group, column_ref[...], 0.0), axis=1, keepdims=True)
    vir_far = row_ref[pl.ds(partner, 1), :]
    occ_far = occ_ref[kpoint_ref[partner, other], slot]
    live_far = slot < count_ref[partner, other]
    far = rows_of(far_refs)
    total = None
    for i in range(occ_slots):
        columns = slice(i * vir_count, (i + 1) * vir_count)
        coulomb = product(own_refs[i][...], far, ((0,), (0,)))
        occ = occ_ref[kpoint_ref[group, block], i] + occ_far
        live = jnp.logical_and(i < count_ref[group, block], live_far)
        scale = jnp.where(live, 1.0, 0.0).astype(jnp.float32)
        amplitude = coulomb * (scale / ((occ - vir_own) - vir_far))
        mixed = (2.0 * amplitude - amplitude.T).astype(jnp.bfloat16)
        if last:
            outs[-1][columns, :] = mixed
        else:
            three = product(far, mixed, ((1,), (1,)))
            outs[-1][:, columns] = three if not sums else sum_refs[1][:, columns] + three
        term = product(mixed, amplitude.astype(jnp.bfloat16), ((1,), (1,)))
        total = term if total is None else total + term
    if sums:
        total = sum_refs[0][...] + total
    if not last:
        outs[0][...] = total
        return
    total = total * scale_by
    if len(outs) == 2:
        outs[0][...] = total
        return
    sent_ref, kept_ref = outs[:2]
    part = vir_count // (wide_count * group_count)
    order = halving_order(wide_count, group_count)
    total = jnp.concatenate([total[part * place : part * (place + 1)] for place in order], axis=0)
    half = vir_count // 2
    low = group % 2 == 0
    sent_ref[...] = jnp.where(low, total[half:], total[:half]).astype(jnp.bfloat16)
    kept_ref[...] = jnp.where(low, total[:half], total[half:])


def gamma_kernel(sum_ref, mixed_ref, *refs):
    far = rows_of(refs[:-1])
    refs[-1][...] = (sum_ref[...] + product(far, mixed_ref[...], ((1,), (1,)))).astype(refs[-1].dtype)


VMEM = pl.BlockSpec(memory_space=pltpu.VMEM)
SMEM = pl.BlockSpec(memory_space=pltpu.SMEM)


def pair_terms(offset, slot, small, own, far, sums, last=False, scale_by=1.0):
    aux_count, vir_count = own[0].shape
    width = len(own) * vir_count
    density = jax.ShapeDtypeStruct((vir_count, vir_count), jnp.float32)
    gamma = jax.ShapeDtypeStruct((aux_count, width), jnp.float32)
    mixed = jax.ShapeDtypeStruct((width, vir_count), jnp.bfloat16)
    halves = [jax.ShapeDtypeStruct((vir_count // 2, vir_count), kind) for kind in (jnp.bfloat16, jnp.float32)]
    split = vir_count % (lax.axis_size("wide") * lax.axis_size("narrow")) == 0
    shapes = ((*halves, mixed) if split else (density, mixed)) if last else (density, gamma)
    sums = sums[:1] if last else sums
    operands = [*small, *own, *far, *sums]
    flops = 4 * aux_count * width * vir_count + 2 * width * vir_count * vir_count
    moved = 2 * aux_count * (width + vir_count) + 8 * vir_count * vir_count + 8 * aux_count * width
    return pl.pallas_call(
        functools.partial(pair_kernel, offset, slot, len(far), len(sums), last, scale_by),
        out_shape=shapes,
        in_specs=[SMEM] * 3 + [VMEM] * (len(operands) - 3),
        out_specs=tuple([VMEM] * len(shapes)),
        compiler_params=pltpu.CompilerParams(vmem_limit_bytes=32 * 1024 * 1024),
        cost_estimate=pl.CostEstimate(flops=flops, bytes_accessed=moved, transcendentals=0),
    )(*operands)


def three_index(gamma, mixed, far):
    aux_count, width = gamma.shape
    vir_count = mixed.shape[1]
    return pl.pallas_call(
        gamma_kernel,
        out_shape=jax.ShapeDtypeStruct((aux_count, width), jnp.bfloat16),
        in_specs=[VMEM] * (2 + len(far)),
        out_specs=VMEM,
        compiler_params=pltpu.CompilerParams(vmem_limit_bytes=32 * 1024 * 1024),
        cost_estimate=pl.CostEstimate(
            flops=2 * aux_count * width * vir_count, bytes_accessed=6 * gamma.size, transcendentals=0
        ),
    )(gamma, mixed, *far)


def halving_stages(wide_count, group_count):
    stages = [("narrow", mask) for mask in reversed(bits_of(group_count))]
    return stages + [("wide", mask) for mask in reversed(bits_of(wide_count))]


def halving_order(wide_count, group_count):
    order = [0]
    for axis, mask in reversed(halving_stages(wide_count, group_count)):
        step = mask * group_count if axis == "wide" else mask
        order = order + [place + step for place in order]
    return order


def halved_sum(sent, kept, beside):
    stages = halving_stages(lax.axis_size("wide"), lax.axis_size("narrow"))
    for position, (axis, mask) in enumerate(stages):
        value = kept + flip(sent, axis, mask).astype(jnp.float32)
        if position + 1 < len(stages):
            axis, mask = stages[position + 1]
            bit = (lax.axis_index(axis) // mask) % 2
            half = value.shape[0] // 2
            sent = lax.dynamic_slice_in_dim(value, (1 - bit) * half, half, 0).astype(jnp.bfloat16)
            kept = lax.dynamic_slice_in_dim(value, bit * half, half, 0)
            sent = after(sent, beside) if position == 1 else sent
    return value.reshape(-1)


def pack_kernel(slot, sets, raw_ref, *outs):
    block = lax.axis_index("wide")
    for offsets, out_ref in zip(sets, outs):
        for place, offset in enumerate(offsets):
            out_ref[place] = raw_ref[:, jnp.bitwise_xor(block, offset), slot, :]


def packed(raw, slot, sets):
    rows, _, _, vir_count = raw.shape
    return pl.pallas_call(
        functools.partial(pack_kernel, slot, sets),
        out_shape=tuple(jax.ShapeDtypeStruct((len(offsets), rows, vir_count), raw.dtype) for offsets in sets),
        in_specs=[VMEM],
        out_specs=tuple([VMEM] * len(sets)),
        compiler_params=pltpu.CompilerParams(vmem_limit_bytes=32 * 1024 * 1024),
        cost_estimate=pl.CostEstimate(flops=0, bytes_accessed=6 * raw.size, transcendentals=0),
    )(raw)


def sent_direct(raw, slot):
    places = doubled(lax.axis_size("wide"))
    places = places[: len(places) // 2]
    messages = packed(raw, slot, [[place, place ^ 1] for place in places])
    arrived = [flip(message, "wide", place) if place else message for message, place in zip(messages, places)]
    return [jnp.concatenate([message[part] for message in arrived], axis=0) for part in range(2)]


def sent_halving(raw, slot, earlier):
    count = lax.axis_size("wide")
    kept, message = packed(raw, slot, [list(range(count // 2)), list(range(count // 2, count))])
    held = {offset: [kept[offset]] for offset in range(count // 2)}
    for mask in bits_of(count)[:-1]:
        if message is None:
            sent = [offset for offset in held if offset & mask]
            message = jnp.stack([piece for offset in sent for piece in held.pop(offset)])
            message = after(message, *earlier)
        pieces = list(flip(message, "wide", mask))
        message = None
        depth = len(pieces) // len(held)
        for place, offset in enumerate(sorted(held)):
            held[offset] = held[offset] + pieces[place * depth : (place + 1) * depth]
    return [jnp.concatenate(held[part], axis=0) for part in range(2)]


def after(value, *earlier):
    return lax.optimization_barrier((value, *earlier))[0]


def gathered_rows(raw, metric):
    wide_count, group_count = lax.axis_size("wide"), lax.axis_size("narrow")
    half_turn = [(source, (source + group_count // 2) % group_count) for source in range(group_count)]
    half = metric.shape[1] // 2
    part = lax.dynamic_slice_in_dim(metric, lax.axis_index("narrow") % 2 * half, half, 1)
    steps = []
    for mask in bits_of(wide_count):
        steps.append(flip(part, "wide", mask))
        part = jnp.concatenate([part, steps[-1]], axis=0)
    metric = [part, flip(part, "narrow", 1)]
    rest = []
    for slot in range(raw.shape[2]):
        if slot:
            mine, theirs = sent_halving(after(raw, mine_sent), slot, [mine])
            mine, theirs = after(mine, *facing_rows), after(theirs, own_rows[1])
        else:
            mine, theirs = sent_direct(raw, slot)
            mine_sent = steps[0]
        first = lax.ppermute(mine, "narrow", half_turn)
        received = flip(theirs, "wide", 1)
        own_rows = [mine, received]
        facing_rows = [first, lax.ppermute(after(received, *facing) if slot else after(received, first), "narrow", half_turn)]
        if slot:
            own += fit(metric, [own_rows], [1])[0]
            rest.append(facing_rows)
        else:
            own, facing = fit(metric, [own_rows, facing_rows], [1, FAR_PARTS])
    return own, facing, metric, rest


def scattered_sum(density):
    wide_count = lax.axis_size("wide")
    group_count = lax.axis_size("narrow")
    wide_bits, narrow_bits = bits_of(wide_count), bits_of(group_count)
    part = density.size // (wide_count * group_count)
    lane = 128 if part % 128 == 0 else part
    value = density.reshape([2] * (len(wide_bits) + len(narrow_bits)) + [part // lane, lane])
    stages = [("narrow", mask, len(wide_bits) + place) for place, mask in enumerate(narrow_bits)]
    stages = stages[::-1] + [("wide", mask, place) for place, mask in reversed(list(enumerate(wide_bits)))]
    for axis, mask, dim in stages:
        bit = (lax.axis_index(axis) // mask) % 2
        sent = lax.dynamic_index_in_dim(value, 1 - bit, dim, keepdims=False).astype(jnp.bfloat16)
        kept = lax.dynamic_index_in_dim(value, bit, dim, keepdims=False)
        value = kept + flip(sent, axis, mask).astype(jnp.float32)
    return value.reshape(-1)


def shards(raw_ints, metric_root, occ_energy, vir_energy, block_kpoint, occ_count):
    _, aux_rows, block_count, occ_slots, vir_count = raw_ints.shape
    wide_count = lax.axis_size("wide")
    group_count = lax.axis_size("narrow")
    my_block = lax.axis_index("wide")
    direct = wide_count <= DIRECT and is_power(wide_count) and wide_count > 2 and group_count % 2 == 0
    small = (occ_energy, block_kpoint, occ_count, vir_energy, vir_energy.T)
    half_turn = [(source, (source + group_count // 2) % group_count) for source in range(group_count)]

    if direct:
        own, facing, metric, rest = gathered_rows(raw_ints[0], metric_root)
    else:
        metric = [lax.all_gather(metric_root, "wide", axis=0, tiled=True)]
        own, rest = [], []
        for slot in range(occ_slots):
            blocks = jnp.transpose(raw_ints[0, :, :, slot, :], (1, 0, 2))
            rows = lax.all_to_all(blocks, "wide", split_axis=0, concat_axis=0, tiled=True)
            rows = rows.reshape(wide_count * aux_rows, vir_count)
            own += fit(metric, [[rows]], [1])[0]
            rest.append([lax.ppermute(rows, "narrow", half_turn)])
        (facing,) = fit(metric, [rest.pop(0)], [FAR_PARTS])
    aux_count = own[0].shape[0]

    pair = functools.partial(pair_terms, small=small, own=own)
    ahead, second, first = [], [], []
    sums = ()
    for slot in range(occ_slots):
        if slot:
            part, *parts = rest[slot - 1]
            (facing,) = fit(metric, [[after(part, *sums), *parts]], [FAR_PARTS])
        ahead.append(facing)
        second.append([from_ahead(part, "wide", 2) for part in facing])
        if slot == 0:
            sums = pair(0, slot, far=facing, sums=sums)
    for slot in range(occ_slots):
        if wide_count % 2 == 0:
            chosen = [choice(after(odd, *sums), even) for odd, even in zip(ahead[slot], second[slot])]
            first.append([flip(part, "wide", 1) for part in chosen])
        else:
            chosen = ()
            first.append([from_ahead(part, "wide", 1) for part in ahead[slot]])
        if slot + 1 < occ_slots:
            sums = pair(0, slot + 1, far=[after(part, *chosen) for part in ahead[slot + 1]], sums=sums)
        sums = pair(2, slot, far=second[slot], sums=sums)
    for slot in range(occ_slots - 1):
        sums = pair(1, slot, far=first[slot], sums=sums)
    norm_scale = 1.0 / (group_count * wide_count * vir_count)
    *terms, mixed = pair(1, occ_slots - 1, far=first[-1], sums=sums, last=True, scale_by=norm_scale)
    gamma = three_index(sums[1], mixed, first[-1])
    if len(terms) == 2:
        virt_density = halved_sum(*terms, gamma)
    else:
        virt_density = scattered_sum(*terms)
    return gamma.reshape(1, aux_count, 1, occ_slots, vir_count), virt_density


def solution(mesh):
    placed = (P("narrow", "wide", None, None, None), P("wide", None), P(), P(), P(), P())
    return jax.shard_map(
        shards,
        mesh=mesh,
        in_specs=placed,
        out_specs=(P("narrow", None, "wide", None, None), P(("wide", "narrow"))),
        check_vma=False,
    )
```

```python
import functools

import jax
import jax.numpy as jnp
from jax import lax
from jax.experimental import pallas as pl
from jax.experimental.pallas import tpu as pltpu
from jax.sharding import PartitionSpec as P

WINDOW = 3
DIRECT = 8
STAGE_BITS = (2, 1, 1)
FAR_PARTS = 1


def flip(value, axis, mask):
    pairs = [(source, source ^ mask) for source in range(lax.axis_size(axis))]
    return lax.ppermute(value, axis, pairs)


def from_ahead(value, axis, steps):
    count = lax.axis_size(axis)
    pairs = [(source, (source - steps) % count) for source in range(count)]
    return lax.ppermute(value, axis, pairs)


def is_power(count):
    return count & (count - 1) == 0


def bits_of(count):
    return [1 << bit for bit in reversed(range(count.bit_length() - 1))]


def doubled(count):
    order = [0]
    for mask in bits_of(count):
        order = order + [place ^ mask for place in order]
    return order


def rows_of(refs):
    return refs[0][...] if len(refs) == 1 else jnp.concatenate([ref[...] for ref in refs], axis=0)


def product(left, right, dims):
    return lax.dot_general(left, right, ((dims[0], dims[1]), ((), ())), preferred_element_type=jnp.float32)


def fit_kernel(halves, parts, cuts, *refs):
    metric_refs, refs = refs[:halves], refs[halves:]
    sources, outs = refs[: parts * len(cuts)], refs[parts * len(cuts) :]
    low = lax.axis_index("narrow") % 2 == 0
    for source, cut in enumerate(cuts):
        rows = rows_of(sources[source * parts : (source + 1) * parts])
        fitted = [product(metric_ref[...], rows, ((0,), (0,))) for metric_ref in metric_refs]
        if halves == 2:
            fitted = [jnp.where(low, fitted[0], fitted[1]), jnp.where(low, fitted[1], fitted[0])]
        fitted = jnp.concatenate([part.astype(outs[0].dtype) for part in fitted], axis=0)
        size = fitted.shape[0] // cut
        for place, out_ref in enumerate(outs[:cut]):
            out_ref[...] = fitted[place * size : (place + 1) * size]
        outs = outs[cut:]


def fit(metric, sources, cuts):
    aux_count = sum(half.shape[1] for half in metric)
    vir_count = sources[0][0].shape[1]
    shapes = [
        jax.ShapeDtypeStruct((aux_count // cut, vir_count), sources[0][0].dtype) for cut in cuts for _ in range(cut)
    ]
    operands = [*metric, *[part for source in sources for part in source]]
    flops = 2 * len(sources) * aux_count * aux_count * vir_count
    moved = 2 * aux_count * (aux_count + 2 * len(sources) * vir_count)
    results = pl.pallas_call(
        functools.partial(fit_kernel, len(metric), len(sources[0]), cuts),
        out_shape=tuple(shapes),
        in_specs=[VMEM] * len(operands),
        out_specs=tuple([VMEM] * len(shapes)),
        compiler_params=pltpu.CompilerParams(vmem_limit_bytes=32 * 1024 * 1024),
        cost_estimate=pl.CostEstimate(flops=flops, bytes_accessed=moved, transcendentals=0),
    )(*operands)
    return [list(results[sum(cuts[:place]) : sum(cuts[: place + 1])]) for place in range(len(cuts))]


def choice_kernel(odd_ref, even_ref, out_ref):
    odd = lax.axis_index("wide") % 2 == 1

    @pl.when(odd)
    def _():
        out_ref[...] = odd_ref[...]

    @pl.when(jnp.logical_not(odd))
    def _():
        out_ref[...] = even_ref[...]


def choice(odd, even):
    return pl.pallas_call(
        choice_kernel,
        out_shape=jax.ShapeDtypeStruct(odd.shape, odd.dtype),
        in_specs=[VMEM] * 2,
        out_specs=VMEM,
        compiler_params=pltpu.CompilerParams(vmem_limit_bytes=32 * 1024 * 1024),
        cost_estimate=pl.CostEstimate(flops=0, bytes_accessed=6 * odd.size, transcendentals=0),
    )(odd, even)


def pair_kernel(offset, slot, fars, sums, wanted, scale_by, *refs):
    occ_ref, kpoint_ref, count_ref, row_ref, column_ref = refs[:5]
    occ_slots = occ_ref.shape[1]
    own_refs, refs = refs[5 : 5 + occ_slots], refs[5 + occ_slots :]
    far_refs, refs = refs[:fars], refs[fars:]
    sum_refs, outs = refs[:sums], refs[sums:]
    group_count, wide_count = kpoint_ref.shape
    vir_count = row_ref.shape[1]
    group = lax.axis_index("narrow")
    block = lax.axis_index("wide")
    partner = lax.rem(group + group_count // 2, group_count)
    other = lax.rem(block + offset, wide_count)
    spot = lax.broadcasted_iota(jnp.int32, column_ref.shape, 1)
    vir_own = jnp.sum(jnp.where(spot == group, column_ref[...], 0.0), axis=1, keepdims=True)
    vir_far = row_ref[pl.ds(partner, 1), :]
    occ_far = occ_ref[kpoint_ref[partner, other], slot]
    live_far = slot < count_ref[partner, other]
    far = rows_of(far_refs)
    total = None
    for i in range(occ_slots):
        columns = slice(i * vir_count, (i + 1) * vir_count)
        coulomb = product(own_refs[i][...], far, ((0,), (0,)))
        occ = occ_ref[kpoint_ref[group, block], i] + occ_far
        live = jnp.logical_and(i < count_ref[group, block], live_far)
        scale = jnp.where(live, 1.0, 0.0).astype(jnp.float32)
        amplitude = coulomb * (scale / ((occ - vir_own) - vir_far))
        mixed = (2.0 * amplitude - amplitude.T).astype(jnp.bfloat16)
        if "gamma" in wanted:
            three = product(far, mixed, ((1,), (1,)))
            three = three if not sums else sum_refs[-1][:, columns] + three
            outs[-1][:, columns] = three.astype(outs[-1].dtype)
        if "density" in wanted:
            term = product(mixed, amplitude.astype(jnp.bfloat16), ((1,), (1,)))
            total = term if total is None else total + term
    if "density" not in wanted:
        return
    if sums:
        total = sum_refs[0][...] + total
    if "gamma" in wanted:
        outs[0][...] = total
        return
    total = total * scale_by
    if len(outs) == 2:
        part = vir_count // (wide_count * group_count)
        order = scatter_order(wide_count, group_count)
        total = jnp.concatenate([total[part * place : part * (place + 1)] for place in order], axis=0)
        split_parts(total, scatter_stages(wide_count, group_count)[0], outs[:1], outs[1])
    else:
        outs[0][...] = total


def split_parts(value, bits, sent_refs, kept_ref):
    count = 2 ** len(bits)
    rows = value.shape[0] // count
    places = [lax.axis_index(axis) // mask % 2 for axis, mask in bits]

    def part(flips):
        candidates = [value[place * rows : (place + 1) * rows] for place in range(count)]
        for position, place in enumerate(places):
            upper = place != (flips >> (len(bits) - 1 - position)) % 2
            half = len(candidates) // 2
            candidates = [jnp.where(upper, high, low) for low, high in zip(candidates[:half], candidates[half:])]
        return candidates[0]

    kept_ref[...] = part(0)
    for flips, sent_ref in enumerate(sent_refs, 1):
        sent_ref[...] = part(flips).astype(sent_ref.dtype)


VMEM = pl.BlockSpec(memory_space=pltpu.VMEM)
SMEM = pl.BlockSpec(memory_space=pltpu.SMEM)


def pair_terms(offset, slot, small, own, far, sums, wanted=("density", "gamma"), scale_by=1.0):
    aux_count, vir_count = own[0].shape
    width = len(own) * vir_count
    density = jax.ShapeDtypeStruct((vir_count, vir_count), jnp.float32)
    halves = [jax.ShapeDtypeStruct((vir_count // 2, vir_count), kind) for kind in (jnp.bfloat16, jnp.float32)]
    if wanted == ("density",):
        whole = vir_count % (lax.axis_size("wide") * lax.axis_size("narrow")) == 0
        shapes, sums = (halves if whole else [density]), sums[:1]
    elif wanted == ("gamma",):
        shapes, sums = [jax.ShapeDtypeStruct((aux_count, width), jnp.bfloat16)], sums[1:]
    else:
        shapes = [density, jax.ShapeDtypeStruct((aux_count, width), jnp.float32)]
    operands = [*small, *own, *far, *sums]
    flops = 4 * aux_count * width * vir_count + 2 * width * vir_count * vir_count
    moved = 2 * aux_count * (width + vir_count) + 8 * vir_count * vir_count + 8 * aux_count * width
    return pl.pallas_call(
        functools.partial(pair_kernel, offset, slot, len(far), len(sums), wanted, scale_by),
        out_shape=tuple(shapes),
        in_specs=[SMEM] * 3 + [VMEM] * (len(operands) - 3),
        out_specs=tuple([VMEM] * len(shapes)),
        compiler_params=pltpu.CompilerParams(vmem_limit_bytes=32 * 1024 * 1024),
        cost_estimate=pl.CostEstimate(flops=flops, bytes_accessed=moved, transcendentals=0),
    )(*operands)


def scatter_stages(wide_count, group_count):
    bits = [("narrow", mask) for mask in reversed(bits_of(group_count))]
    bits += [("wide", mask) for mask in reversed(bits_of(wide_count))]
    stages = [bits[:1]]
    for size in STAGE_BITS:
        stages.append(bits[sum(map(len, stages)) :][:size])
    stages.append(bits[sum(map(len, stages)) :])
    return [stage for stage in stages if stage]


def scatter_order(wide_count, group_count):
    order = [0]
    for axis, mask in reversed([bit for stage in scatter_stages(wide_count, group_count) for bit in stage]):
        step = mask * group_count if axis == "wide" else mask
        order = order + [place + step for place in order]
    return order


def flipped(value, bits, flips):
    group_count = lax.axis_size("narrow")
    masks = [mask * group_count if axis == "wide" else mask for axis, mask in bits]
    step = sum(mask for place, mask in enumerate(reversed(masks)) if flips >> place & 1)
    if len(bits) == 1:
        return flip(value, *bits[0])
    pairs = [(source, source ^ step) for source in range(lax.axis_size("wide") * group_count)]
    return lax.ppermute(value, ("wide", "narrow"), pairs)


def scatter_kernel(bits, got_count, *refs):
    value = refs[got_count][...]
    for got_ref in refs[:got_count]:
        value = value + got_ref[...].astype(jnp.float32)
    outs = refs[got_count + 1 :]
    if bits:
        split_parts(value, bits, outs[:-1], outs[-1])
    elif outs[0].shape == value.shape:
        outs[0][...] = value
    else:
        lanes = outs[0].shape[1]
        tiles = value.shape[1] // lanes
        for tile in range(tiles):
            outs[0][pl.ds(tile, value.shape[0], tiles), :] = value[:, tile * lanes : (tile + 1) * lanes]


def scattered_parts(sent, kept, beside):
    stages = scatter_stages(lax.axis_size("wide"), lax.axis_size("narrow"))
    sents = [sent]
    for position, bits in enumerate(stages):
        rows, columns = kept.shape
        following = stages[position + 1] if position + 1 < len(stages) else []
        if following:
            part = (rows // 2 ** len(following), columns)
            shapes = [jax.ShapeDtypeStruct(part, sent.dtype)] * (2 ** len(following) - 1)
            shapes.append(jax.ShapeDtypeStruct(part, kept.dtype))
        else:
            lanes = 128 if columns % 128 == 0 else columns
            shapes = [jax.ShapeDtypeStruct((rows * columns // lanes, lanes), kept.dtype)]
        got = [flipped(value, bits, flips) for flips, value in enumerate(sents, 1)]
        *sents, kept = pl.pallas_call(
            functools.partial(scatter_kernel, following, len(got)),
            out_shape=tuple(shapes),
            in_specs=[VMEM] * (len(got) + 1),
            out_specs=tuple([VMEM] * len(shapes)),
            compiler_params=pltpu.CompilerParams(vmem_limit_bytes=8 * 1024 * 1024),
            cost_estimate=pl.CostEstimate(flops=rows * columns, bytes_accessed=8 * rows * columns, transcendentals=0),
        )(*got, kept)
        if position == 1:
            sents = [after(value, beside) for value in sents]
    return kept.reshape(-1)


def pack_kernel(slot, sets, raw_ref, *outs):
    block = lax.axis_index("wide")
    for offsets, out_ref in zip(sets, outs):
        for place, offset in enumerate(offsets):
            out_ref[place] = raw_ref[:, jnp.bitwise_xor(block, offset), slot, :]


def packed(raw, slot, sets):
    rows, _, _, vir_count = raw.shape
    return pl.pallas_call(
        functools.partial(pack_kernel, slot, sets),
        out_shape=tuple(jax.ShapeDtypeStruct((len(offsets), rows, vir_count), raw.dtype) for offsets in sets),
        in_specs=[VMEM],
        out_specs=tuple([VMEM] * len(sets)),
        compiler_params=pltpu.CompilerParams(vmem_limit_bytes=32 * 1024 * 1024),
        cost_estimate=pl.CostEstimate(flops=0, bytes_accessed=6 * raw.size, transcendentals=0),
    )(raw)


def sent_direct(raw, slot):
    places = doubled(lax.axis_size("wide"))
    places = places[: len(places) // 2]
    messages = packed(raw, slot, [[place, place ^ 1] for place in places])
    arrived = [flip(message, "wide", place) if place else message for message, place in zip(messages, places)]
    return [jnp.concatenate([message[part] for message in arrived], axis=0) for part in range(2)]


def sent_halving(raw, slot):
    count = lax.axis_size("wide")
    masks = bits_of(count)[-2::-1]
    sets = [[offset for offset in range(count) if offset & masks[0] == sent] for sent in (0, masks[0])]
    kept, message = packed(raw, slot, sets)
    held = {offset: {0: piece} for offset, piece in zip(sets[0], kept)}
    for mask in masks:
        if message is None:
            sent = [held.pop(offset) for offset in sorted(held) if offset & mask]
            message = jnp.stack([piece for pieces in sent for piece in pieces.values()])
        pieces = iter(flip(message, "wide", mask))
        message = None
        for offset in sorted(held):
            held[offset].update({place ^ mask: next(pieces) for place in list(held[offset])})
    order = doubled(count)[: count // 2]
    return [jnp.concatenate([held[part][place] for place in order], axis=0) for part in range(2)]


def after(value, *earlier):
    return lax.optimization_barrier((value, *earlier))[0]


def gathered_rows(raw, metric):
    wide_count, group_count = lax.axis_size("wide"), lax.axis_size("narrow")
    half_turn = [(source, (source + group_count // 2) % group_count) for source in range(group_count)]
    half = metric.shape[1] // 2
    part = lax.dynamic_slice_in_dim(metric, lax.axis_index("narrow") % 2 * half, half, 1)
    steps = []
    for mask in bits_of(wide_count):
        steps.append(flip(part, "wide", mask))
        part = jnp.concatenate([part, steps[-1]], axis=0)
    metric = [part, flip(part, "narrow", 1)]
    rest = []
    for slot in range(raw.shape[2]):
        if slot:
            mine, theirs = sent_halving(after(raw, mine_sent), slot)
            mine, theirs = after(mine, *facing_rows), after(theirs, own_rows[1])
        else:
            mine, theirs = sent_direct(raw, slot)
            mine_sent = steps[0]
        first = lax.ppermute(mine, "narrow", half_turn)
        received = flip(theirs, "wide", 1)
        own_rows = [mine, received]
        facing_rows = [first, lax.ppermute(after(received, *facing) if slot else received, "narrow", half_turn)]
        if slot:
            own += fit(metric, [own_rows], [1])[0]
            rest.append(facing_rows)
        else:
            own, facing = fit(metric, [own_rows, facing_rows], [1, FAR_PARTS])
    return own, facing, metric, rest


def scattered_sum(density):
    wide_count = lax.axis_size("wide")
    group_count = lax.axis_size("narrow")
    wide_bits, narrow_bits = bits_of(wide_count), bits_of(group_count)
    part = density.size // (wide_count * group_count)
    lane = 128 if part % 128 == 0 else part
    value = density.reshape([2] * (len(wide_bits) + len(narrow_bits)) + [part // lane, lane])
    stages = [("narrow", mask, len(wide_bits) + place) for place, mask in enumerate(narrow_bits)]
    stages = stages[::-1] + [("wide", mask, place) for place, mask in reversed(list(enumerate(wide_bits)))]
    for axis, mask, dim in stages:
        bit = (lax.axis_index(axis) // mask) % 2
        sent = lax.dynamic_index_in_dim(value, 1 - bit, dim, keepdims=False).astype(jnp.bfloat16)
        kept = lax.dynamic_index_in_dim(value, bit, dim, keepdims=False)
        value = kept + flip(sent, axis, mask).astype(jnp.float32)
    return value.reshape(-1)


def shards(raw_ints, metric_root, occ_energy, vir_energy, block_kpoint, occ_count):
    _, aux_rows, block_count, occ_slots, vir_count = raw_ints.shape
    wide_count = lax.axis_size("wide")
    group_count = lax.axis_size("narrow")
    my_block = lax.axis_index("wide")
    direct = wide_count <= DIRECT and is_power(wide_count) and wide_count > 2 and group_count % 2 == 0
    small = (occ_energy, block_kpoint, occ_count, vir_energy, vir_energy.T)
    half_turn = [(source, (source + group_count // 2) % group_count) for source in range(group_count)]

    if direct:
        own, facing, metric, rest = gathered_rows(raw_ints[0], metric_root)
    else:
        metric = [lax.all_gather(metric_root, "wide", axis=0, tiled=True)]
        own, rest = [], []
        for slot in range(occ_slots):
            blocks = jnp.transpose(raw_ints[0, :, :, slot, :], (1, 0, 2))
            rows = lax.all_to_all(blocks, "wide", split_axis=0, concat_axis=0, tiled=True)
            rows = rows.reshape(wide_count * aux_rows, vir_count)
            own += fit(metric, [[rows]], [1])[0]
            rest.append([lax.ppermute(rows, "narrow", half_turn)])
        (facing,) = fit(metric, [rest.pop(0)], [FAR_PARTS])
    aux_count = own[0].shape[0]

    pair = functools.partial(pair_terms, small=small, own=own)
    ahead, second, first = [], [], []
    sums = ()
    for slot in range(occ_slots):
        if slot:
            part, *parts = rest[slot - 1]
            (facing,) = fit(metric, [[after(part, *sums), *parts]], [FAR_PARTS])
        ahead.append(facing)
        second.append([from_ahead(part, "wide", 2) for part in facing])
        if slot == 0:
            sums = pair(0, slot, far=facing, sums=sums)
    for slot in range(occ_slots):
        if wide_count % 2 == 0:
            chosen = [choice(after(odd, *sums), even) for odd, even in zip(ahead[slot], second[slot])]
            first.append([flip(part, "wide", 1) for part in chosen])
        else:
            chosen = ()
            first.append([from_ahead(part, "wide", 1) for part in ahead[slot]])
        if slot + 1 < occ_slots:
            sums = pair(0, slot + 1, far=[after(part, *chosen) for part in ahead[slot + 1]], sums=sums)
        sums = pair(2, slot, far=second[slot], sums=sums)
    for slot in range(occ_slots - 1):
        sums = pair(1, slot, far=first[slot], sums=sums)
    norm_scale = 1.0 / (group_count * wide_count * vir_count)
    last = functools.partial(pair, 1, occ_slots - 1, far=first[-1], sums=sums)
    terms = last(wanted=("density",), scale_by=norm_scale)
    (gamma,) = last(wanted=("gamma",))
    if len(terms) == 2:
        virt_density = scattered_parts(*terms, gamma)
    else:
        virt_density = scattered_sum(*terms)
    return gamma.reshape(1, aux_count, 1, occ_slots, vir_count), virt_density


def solution(mesh):
    placed = (P("narrow", "wide", None, None, None), P("wide", None), P(), P(), P(), P())
    return jax.shard_map(
        shards,
        mesh=mesh,
        in_specs=placed,
        out_specs=(P("narrow", None, "wide", None, None), P(("wide", "narrow"))),
        check_vma=False,
    )
```

```python
import functools

import jax
import jax.numpy as jnp
from jax import lax
from jax.experimental import pallas as pl
from jax.experimental.pallas import tpu as pltpu
from jax.sharding import PartitionSpec as P

WINDOW = 3
DIRECT = 8
STAGE_BITS = (2, 1, 1)
FAR_PARTS = 1


def flip(value, axis, mask):
    pairs = [(source, source ^ mask) for source in range(lax.axis_size(axis))]
    return lax.ppermute(value, axis, pairs)


def from_ahead(value, axis, steps):
    count = lax.axis_size(axis)
    pairs = [(source, (source - steps) % count) for source in range(count)]
    return lax.ppermute(value, axis, pairs)


def is_power(count):
    return count & (count - 1) == 0


def bits_of(count):
    return [1 << bit for bit in reversed(range(count.bit_length() - 1))]


def doubled(count):
    order = [0]
    for mask in bits_of(count):
        order = order + [place ^ mask for place in order]
    return order


def rows_of(refs):
    return refs[0][...] if len(refs) == 1 else jnp.concatenate([ref[...] for ref in refs], axis=0)


def product(left, right, dims):
    return lax.dot_general(left, right, ((dims[0], dims[1]), ((), ())), preferred_element_type=jnp.float32)


def fit_kernel(halves, parts, cuts, *refs):
    metric_refs, refs = refs[:halves], refs[halves:]
    sources, outs = refs[: parts * len(cuts)], refs[parts * len(cuts) :]
    low = lax.axis_index("narrow") % 2 == 0
    for source, cut in enumerate(cuts):
        rows = rows_of(sources[source * parts : (source + 1) * parts])
        fitted = [product(metric_ref[...], rows, ((0,), (0,))) for metric_ref in metric_refs]
        if halves == 2:
            fitted = [jnp.where(low, fitted[0], fitted[1]), jnp.where(low, fitted[1], fitted[0])]
        fitted = jnp.concatenate([part.astype(outs[0].dtype) for part in fitted], axis=0)
        size = fitted.shape[0] // cut
        for place, out_ref in enumerate(outs[:cut]):
            out_ref[...] = fitted[place * size : (place + 1) * size]
        outs = outs[cut:]


def fit(metric, sources, cuts):
    aux_count = sum(half.shape[1] for half in metric)
    vir_count = sources[0][0].shape[1]
    shapes = [
        jax.ShapeDtypeStruct((aux_count // cut, vir_count), sources[0][0].dtype) for cut in cuts for _ in range(cut)
    ]
    operands = [*metric, *[part for source in sources for part in source]]
    flops = 2 * len(sources) * aux_count * aux_count * vir_count
    moved = 2 * aux_count * (aux_count + 2 * len(sources) * vir_count)
    results = pl.pallas_call(
        functools.partial(fit_kernel, len(metric), len(sources[0]), cuts),
        out_shape=tuple(shapes),
        in_specs=[VMEM] * len(operands),
        out_specs=tuple([VMEM] * len(shapes)),
        compiler_params=pltpu.CompilerParams(vmem_limit_bytes=32 * 1024 * 1024),
        cost_estimate=pl.CostEstimate(flops=flops, bytes_accessed=moved, transcendentals=0),
    )(*operands)
    return [list(results[sum(cuts[:place]) : sum(cuts[: place + 1])]) for place in range(len(cuts))]


def choice_kernel(odd_ref, even_ref, out_ref):
    odd = lax.axis_index("wide") % 2 == 1

    @pl.when(odd)
    def _():
        out_ref[...] = odd_ref[...]

    @pl.when(jnp.logical_not(odd))
    def _():
        out_ref[...] = even_ref[...]


def choice(odd, even):
    return pl.pallas_call(
        choice_kernel,
        out_shape=jax.ShapeDtypeStruct(odd.shape, odd.dtype),
        in_specs=[VMEM] * 2,
        out_specs=VMEM,
        compiler_params=pltpu.CompilerParams(vmem_limit_bytes=32 * 1024 * 1024),
        cost_estimate=pl.CostEstimate(flops=0, bytes_accessed=6 * odd.size, transcendentals=0),
    )(odd, even)


def pair_kernel(offset, slot, fars, sums, wanted, scale_by, *refs):
    occ_ref, kpoint_ref, count_ref, row_ref, column_ref = refs[:5]
    occ_slots = occ_ref.shape[1]
    own_refs, refs = refs[5 : 5 + occ_slots], refs[5 + occ_slots :]
    far_refs, refs = refs[:fars], refs[fars:]
    sum_refs, outs = refs[:sums], refs[sums:]
    group_count, wide_count = kpoint_ref.shape
    vir_count = row_ref.shape[1]
    group = lax.axis_index("narrow")
    block = lax.axis_index("wide")
    partner = lax.rem(group + group_count // 2, group_count)
    other = lax.rem(block + offset, wide_count)
    spot = lax.broadcasted_iota(jnp.int32, column_ref.shape, 1)
    vir_own = jnp.sum(jnp.where(spot == group, column_ref[...], 0.0), axis=1, keepdims=True)
    vir_far = row_ref[pl.ds(partner, 1), :]
    occ_far = occ_ref[kpoint_ref[partner, other], slot]
    live_far = slot < count_ref[partner, other]
    far = rows_of(far_refs)
    total = None
    for i in range(occ_slots):
        columns = slice(i * vir_count, (i + 1) * vir_count)
        coulomb = product(own_refs[i][...], far, ((0,), (0,)))
        occ = occ_ref[kpoint_ref[group, block], i] + occ_far
        live = jnp.logical_and(i < count_ref[group, block], live_far)
        scale = jnp.where(live, 1.0, 0.0).astype(jnp.float32)
        amplitude = coulomb * (scale / ((occ - vir_own) - vir_far))
        mixed = (2.0 * amplitude - amplitude.T).astype(jnp.bfloat16)
        if "gamma" in wanted:
            three = product(far, mixed, ((1,), (1,)))
            three = three if not sums else sum_refs[-1][:, columns] + three
            outs[-1][:, columns] = three.astype(outs[-1].dtype)
        if "density" in wanted:
            term = product(mixed, amplitude.astype(jnp.bfloat16), ((1,), (1,)))
            total = term if total is None else total + term
    if "density" not in wanted:
        return
    if sums:
        total = sum_refs[0][...] + total
    if "gamma" in wanted:
        outs[0][...] = total
        return
    total = total * scale_by
    if len(outs) == 2:
        part = vir_count // (wide_count * group_count)
        order = scatter_order(wide_count, group_count)
        total = jnp.concatenate([total[part * place : part * (place + 1)] for place in order], axis=0)
        split_parts(total, scatter_stages(wide_count, group_count)[0], outs[:1], outs[1])
    else:
        outs[0][...] = total


def split_parts(value, bits, sent_refs, kept_ref):
    count = 2 ** len(bits)
    rows = value.shape[0] // count
    places = [lax.axis_index(axis) // mask % 2 for axis, mask in bits]

    def part(flips):
        candidates = [value[place * rows : (place + 1) * rows] for place in range(count)]
        for position, place in enumerate(places):
            upper = place != (flips >> (len(bits) - 1 - position)) % 2
            half = len(candidates) // 2
            candidates = [jnp.where(upper, high, low) for low, high in zip(candidates[:half], candidates[half:])]
        return candidates[0]

    kept_ref[...] = part(0)
    for flips, sent_ref in enumerate(sent_refs, 1):
        sent_ref[...] = part(flips).astype(sent_ref.dtype)


VMEM = pl.BlockSpec(memory_space=pltpu.VMEM)
SMEM = pl.BlockSpec(memory_space=pltpu.SMEM)


def pair_terms(offset, slot, small, own, far, sums, wanted=("density", "gamma"), scale_by=1.0, weight=1):
    aux_count, vir_count = own[0].shape
    width = len(own) * vir_count
    density = jax.ShapeDtypeStruct((vir_count, vir_count), jnp.float32)
    halves = [jax.ShapeDtypeStruct((vir_count // 2, vir_count), kind) for kind in (jnp.bfloat16, jnp.float32)]
    if wanted == ("density",):
        whole = vir_count % (lax.axis_size("wide") * lax.axis_size("narrow")) == 0
        shapes, sums = (halves if whole else [density]), sums[:1]
    elif wanted == ("gamma",):
        shapes, sums = [jax.ShapeDtypeStruct((aux_count, width), jnp.bfloat16)], sums[1:]
    else:
        shapes = [density, jax.ShapeDtypeStruct((aux_count, width), jnp.float32)]
    operands = [*small, *own, *far, *sums]
    flops = weight * (4 * aux_count * width * vir_count + 2 * width * vir_count * vir_count)
    moved = weight * (2 * aux_count * (width + vir_count) + 8 * vir_count * vir_count + 8 * aux_count * width)
    return pl.pallas_call(
        functools.partial(pair_kernel, offset, slot, len(far), len(sums), wanted, scale_by),
        out_shape=tuple(shapes),
        in_specs=[SMEM] * 3 + [VMEM] * (len(operands) - 3),
        out_specs=tuple([VMEM] * len(shapes)),
        compiler_params=pltpu.CompilerParams(vmem_limit_bytes=32 * 1024 * 1024),
        cost_estimate=pl.CostEstimate(flops=flops, bytes_accessed=moved, transcendentals=0),
    )(*operands)


def scatter_stages(wide_count, group_count):
    bits = [("narrow", mask) for mask in reversed(bits_of(group_count))]
    bits += [("wide", mask) for mask in reversed(bits_of(wide_count))]
    stages = [bits[:1]]
    for size in STAGE_BITS:
        stages.append(bits[sum(map(len, stages)) :][:size])
    stages.append(bits[sum(map(len, stages)) :])
    return [stage for stage in stages if stage]


def scatter_order(wide_count, group_count):
    order = [0]
    for axis, mask in reversed([bit for stage in scatter_stages(wide_count, group_count) for bit in stage]):
        step = mask * group_count if axis == "wide" else mask
        order = order + [place + step for place in order]
    return order


def flipped(value, bits, flips):
    group_count = lax.axis_size("narrow")
    masks = [mask * group_count if axis == "wide" else mask for axis, mask in bits]
    step = sum(mask for place, mask in enumerate(reversed(masks)) if flips >> place & 1)
    if len(bits) == 1:
        return flip(value, *bits[0])
    pairs = [(source, source ^ step) for source in range(lax.axis_size("wide") * group_count)]
    return lax.ppermute(value, ("wide", "narrow"), pairs)


def scatter_kernel(bits, got_count, *refs):
    value = refs[got_count][...]
    for got_ref in refs[:got_count]:
        value = value + got_ref[...].astype(jnp.float32)
    outs = refs[got_count + 1 :]
    if bits:
        split_parts(value, bits, outs[:-1], outs[-1])
    elif outs[0].shape == value.shape:
        outs[0][...] = value
    else:
        lanes = outs[0].shape[1]
        tiles = value.shape[1] // lanes
        for tile in range(tiles):
            outs[0][pl.ds(tile, value.shape[0], tiles), :] = value[:, tile * lanes : (tile + 1) * lanes]


def scattered_parts(sent, kept, beside):
    stages = scatter_stages(lax.axis_size("wide"), lax.axis_size("narrow"))
    sents = [sent]
    for position, bits in enumerate(stages):
        rows, columns = kept.shape
        following = stages[position + 1] if position + 1 < len(stages) else []
        if following:
            part = (rows // 2 ** len(following), columns)
            shapes = [jax.ShapeDtypeStruct(part, sent.dtype)] * (2 ** len(following) - 1)
            shapes.append(jax.ShapeDtypeStruct(part, kept.dtype))
        else:
            lanes = 128 if columns % 128 == 0 else columns
            shapes = [jax.ShapeDtypeStruct((rows * columns // lanes, lanes), kept.dtype)]
        got = [flipped(value, bits, flips) for flips, value in enumerate(sents, 1)]
        *sents, kept = pl.pallas_call(
            functools.partial(scatter_kernel, following, len(got)),
            out_shape=tuple(shapes),
            in_specs=[VMEM] * (len(got) + 1),
            out_specs=tuple([VMEM] * len(shapes)),
            compiler_params=pltpu.CompilerParams(vmem_limit_bytes=8 * 1024 * 1024),
            cost_estimate=pl.CostEstimate(flops=rows * columns, bytes_accessed=8 * rows * columns, transcendentals=0),
        )(*got, kept)
        if position == 1:
            sents = [after(value, beside) for value in sents]
    return kept.reshape(-1)


def pack_kernel(slot, sets, raw_ref, *outs):
    block = lax.axis_index("wide")
    for offsets, out_ref in zip(sets, outs):
        for place, offset in enumerate(offsets):
            out_ref[place] = raw_ref[:, jnp.bitwise_xor(block, offset), slot, :]


def packed(raw, slot, sets):
    rows, _, _, vir_count = raw.shape
    return pl.pallas_call(
        functools.partial(pack_kernel, slot, sets),
        out_shape=tuple(jax.ShapeDtypeStruct((len(offsets), rows, vir_count), raw.dtype) for offsets in sets),
        in_specs=[VMEM],
        out_specs=tuple([VMEM] * len(sets)),
        compiler_params=pltpu.CompilerParams(vmem_limit_bytes=32 * 1024 * 1024),
        cost_estimate=pl.CostEstimate(flops=0, bytes_accessed=6 * raw.size, transcendentals=0),
    )(raw)


def sent_direct(raw, slot):
    places = doubled(lax.axis_size("wide"))
    places = places[: len(places) // 2]
    messages = packed(raw, slot, [[place, place ^ 1] for place in places])
    arrived = [flip(message, "wide", place) if place else message for message, place in zip(messages, places)]
    return [jnp.concatenate([message[part] for message in arrived], axis=0) for part in range(2)]


def sent_halving(raw, slot):
    count = lax.axis_size("wide")
    masks = bits_of(count)[-2::-1]
    sets = [[offset for offset in range(count) if offset & masks[0] == sent] for sent in (0, masks[0])]
    kept, message = packed(raw, slot, sets)
    held = {offset: {0: piece} for offset, piece in zip(sets[0], kept)}
    for mask in masks:
        if message is None:
            sent = [held.pop(offset) for offset in sorted(held) if offset & mask]
            message = jnp.stack([piece for pieces in sent for piece in pieces.values()])
        pieces = iter(flip(message, "wide", mask))
        message = None
        for offset in sorted(held):
            held[offset].update({place ^ mask: next(pieces) for place in list(held[offset])})
    order = doubled(count)[: count // 2]
    return [jnp.concatenate([held[part][place] for place in order], axis=0) for part in range(2)]


def after(value, *earlier):
    return lax.optimization_barrier((value, *earlier))[0]


def gathered_rows(raw, metric):
    wide_count, group_count = lax.axis_size("wide"), lax.axis_size("narrow")
    half_turn = [(source, (source + group_count // 2) % group_count) for source in range(group_count)]
    half = metric.shape[1] // 2
    part = lax.dynamic_slice_in_dim(metric, lax.axis_index("narrow") % 2 * half, half, 1)
    steps = []
    for mask in bits_of(wide_count):
        steps.append(flip(part, "wide", mask))
        part = jnp.concatenate([part, steps[-1]], axis=0)
    metric = [part, flip(part, "narrow", 1)]
    rest = []
    for slot in range(raw.shape[2]):
        if slot:
            mine, theirs = sent_halving(after(raw, mine_sent), slot)
            mine, theirs = after(mine, *facing_rows), after(theirs, own_rows[1])
        else:
            mine, theirs = sent_direct(raw, slot)
            mine_sent = steps[0]
        first = lax.ppermute(mine, "narrow", half_turn)
        received = flip(theirs, "wide", 1)
        own_rows = [mine, received]
        facing_rows = [first, lax.ppermute(after(received, *facing) if slot else received, "narrow", half_turn)]
        if slot:
            own += fit(metric, [own_rows], [1])[0]
            rest.append(facing_rows)
        else:
            own, facing = fit(metric, [own_rows, facing_rows], [1, FAR_PARTS])
    return own, facing, metric, rest


def scattered_sum(density):
    wide_count = lax.axis_size("wide")
    group_count = lax.axis_size("narrow")
    wide_bits, narrow_bits = bits_of(wide_count), bits_of(group_count)
    part = density.size // (wide_count * group_count)
    lane = 128 if part % 128 == 0 else part
    value = density.reshape([2] * (len(wide_bits) + len(narrow_bits)) + [part // lane, lane])
    stages = [("narrow", mask, len(wide_bits) + place) for place, mask in enumerate(narrow_bits)]
    stages = stages[::-1] + [("wide", mask, place) for place, mask in reversed(list(enumerate(wide_bits)))]
    for axis, mask, dim in stages:
        bit = (lax.axis_index(axis) // mask) % 2
        sent = lax.dynamic_index_in_dim(value, 1 - bit, dim, keepdims=False).astype(jnp.bfloat16)
        kept = lax.dynamic_index_in_dim(value, bit, dim, keepdims=False)
        value = kept + flip(sent, axis, mask).astype(jnp.float32)
    return value.reshape(-1)


def shards(raw_ints, metric_root, occ_energy, vir_energy, block_kpoint, occ_count):
    _, aux_rows, block_count, occ_slots, vir_count = raw_ints.shape
    wide_count = lax.axis_size("wide")
    group_count = lax.axis_size("narrow")
    my_block = lax.axis_index("wide")
    direct = wide_count <= DIRECT and is_power(wide_count) and wide_count > 2 and group_count % 2 == 0
    small = (occ_energy, block_kpoint, occ_count, vir_energy, vir_energy.T)
    half_turn = [(source, (source + group_count // 2) % group_count) for source in range(group_count)]

    if direct:
        own, facing, metric, rest = gathered_rows(raw_ints[0], metric_root)
    else:
        metric = [lax.all_gather(metric_root, "wide", axis=0, tiled=True)]
        own, rest = [], []
        for slot in range(occ_slots):
            blocks = jnp.transpose(raw_ints[0, :, :, slot, :], (1, 0, 2))
            rows = lax.all_to_all(blocks, "wide", split_axis=0, concat_axis=0, tiled=True)
            rows = rows.reshape(wide_count * aux_rows, vir_count)
            own += fit(metric, [[rows]], [1])[0]
            rest.append([lax.ppermute(rows, "narrow", half_turn)])
        (facing,) = fit(metric, [rest.pop(0)], [FAR_PARTS])
    aux_count = own[0].shape[0]

    pair = functools.partial(pair_terms, small=small, own=own)
    ahead, second, first = [], [], []
    sums = ()
    for slot in range(occ_slots):
        if slot:
            part, *parts = rest[slot - 1]
            (facing,) = fit(metric, [[after(part, *sums), *parts]], [FAR_PARTS])
        ahead.append(facing)
        second.append([from_ahead(part, "wide", 2) for part in facing])
        if slot == 0:
            sums = pair(0, slot, far=facing, sums=sums, weight=8)
    for slot in range(occ_slots):
        if wide_count % 2 == 0:
            chosen = [choice(after(odd, *sums), even) for odd, even in zip(ahead[slot], second[slot])]
            first.append([flip(part, "wide", 1) for part in chosen])
        else:
            chosen = ()
            first.append([from_ahead(part, "wide", 1) for part in ahead[slot]])
        if slot + 1 < occ_slots:
            sums = pair(0, slot + 1, far=[after(part, *chosen) for part in ahead[slot + 1]], sums=sums)
        sums = pair(2, slot, far=second[slot], sums=sums)
    for slot in range(occ_slots - 1):
        sums = pair(1, slot, far=first[slot], sums=sums)
    norm_scale = 1.0 / (group_count * wide_count * vir_count)
    last = functools.partial(pair, 1, occ_slots - 1, far=first[-1], sums=sums)
    terms = last(wanted=("density",), scale_by=norm_scale)
    (gamma,) = last(wanted=("gamma",))
    if len(terms) == 2:
        virt_density = scattered_parts(*terms, gamma)
    else:
        virt_density = scattered_sum(*terms)
    return gamma.reshape(1, aux_count, 1, occ_slots, vir_count), virt_density


def solution(mesh):
    placed = (P("narrow", "wide", None, None, None), P("wide", None), P(), P(), P(), P())
    return jax.shard_map(
        shards,
        mesh=mesh,
        in_specs=placed,
        out_specs=(P("narrow", None, "wide", None, None), P(("wide", "narrow"))),
        check_vma=False,
    )
```

```python
import functools

import jax
import jax.numpy as jnp
from jax import lax
from jax.experimental import pallas as pl
from jax.experimental.pallas import tpu as pltpu
from jax.sharding import PartitionSpec as P

WINDOW = 3
DIRECT = 8
STAGE_BITS = (2, 1, 1)
LAST_PARTS = 2


def flip(value, axis, mask):
    pairs = [(source, source ^ mask) for source in range(lax.axis_size(axis))]
    return lax.ppermute(value, axis, pairs)


def from_ahead(value, axis, steps):
    count = lax.axis_size(axis)
    pairs = [(source, (source - steps) % count) for source in range(count)]
    return lax.ppermute(value, axis, pairs)


def is_power(count):
    return count & (count - 1) == 0


def bits_of(count):
    return [1 << bit for bit in reversed(range(count.bit_length() - 1))]


def doubled(count):
    order = [0]
    for mask in bits_of(count):
        order = order + [place ^ mask for place in order]
    return order


def rows_of(refs):
    return refs[0][...] if len(refs) == 1 else jnp.concatenate([ref[...] for ref in refs], axis=0)


def product(left, right, dims):
    return lax.dot_general(left, right, ((dims[0], dims[1]), ((), ())), preferred_element_type=jnp.float32)


def fit_kernel(halves, parts, cuts, *refs):
    metric_refs, refs = refs[:halves], refs[halves:]
    sources, outs = refs[: parts * len(cuts)], refs[parts * len(cuts) :]
    low = lax.axis_index("narrow") % 2 == 0
    for source, cut in enumerate(cuts):
        rows = rows_of(sources[source * parts : (source + 1) * parts])
        fitted = [product(metric_ref[...], rows, ((0,), (0,))) for metric_ref in metric_refs]
        if halves == 2:
            fitted = [jnp.where(low, fitted[0], fitted[1]), jnp.where(low, fitted[1], fitted[0])]
        fitted = jnp.concatenate([part.astype(outs[0].dtype) for part in fitted], axis=0)
        size = fitted.shape[0] // cut
        for place, out_ref in enumerate(outs[:cut]):
            out_ref[...] = fitted[place * size : (place + 1) * size]
        outs = outs[cut:]


def fit(metric, sources, cuts):
    aux_count = sum(half.shape[1] for half in metric)
    vir_count = sources[0][0].shape[1]
    shapes = [
        jax.ShapeDtypeStruct((aux_count // cut, vir_count), sources[0][0].dtype) for cut in cuts for _ in range(cut)
    ]
    operands = [*metric, *[part for source in sources for part in source]]
    flops = 2 * len(sources) * aux_count * aux_count * vir_count
    moved = 2 * aux_count * (aux_count + 2 * len(sources) * vir_count)
    results = pl.pallas_call(
        functools.partial(fit_kernel, len(metric), len(sources[0]), cuts),
        out_shape=tuple(shapes),
        in_specs=[VMEM] * len(operands),
        out_specs=tuple([VMEM] * len(shapes)),
        compiler_params=pltpu.CompilerParams(vmem_limit_bytes=32 * 1024 * 1024),
        cost_estimate=pl.CostEstimate(flops=flops, bytes_accessed=moved, transcendentals=0),
    )(*operands)
    return [list(results[sum(cuts[:place]) : sum(cuts[: place + 1])]) for place in range(len(cuts))]


def choice_kernel(odd_ref, even_ref, out_ref):
    odd = lax.axis_index("wide") % 2 == 1

    @pl.when(odd)
    def _():
        out_ref[...] = odd_ref[...]

    @pl.when(jnp.logical_not(odd))
    def _():
        out_ref[...] = even_ref[...]


def choice(odd, even):
    return pl.pallas_call(
        choice_kernel,
        out_shape=jax.ShapeDtypeStruct(odd.shape, odd.dtype),
        in_specs=[VMEM] * 2,
        out_specs=VMEM,
        compiler_params=pltpu.CompilerParams(vmem_limit_bytes=32 * 1024 * 1024),
        cost_estimate=pl.CostEstimate(flops=0, bytes_accessed=6 * odd.size, transcendentals=0),
    )(odd, even)


def pair_kernel(offset, slot, fars, sums, wanted, scale_by, *refs):
    occ_ref, kpoint_ref, count_ref, row_ref, column_ref = refs[:5]
    occ_slots = occ_ref.shape[1]
    own_refs, refs = refs[5 : 5 + occ_slots], refs[5 + occ_slots :]
    far_refs, refs = refs[:fars], refs[fars:]
    sum_refs, outs = refs[:sums], refs[sums:]
    group_count, wide_count = kpoint_ref.shape
    vir_count = row_ref.shape[1]
    group = lax.axis_index("narrow")
    block = lax.axis_index("wide")
    partner = lax.rem(group + group_count // 2, group_count)
    other = lax.rem(block + offset, wide_count)
    spot = lax.broadcasted_iota(jnp.int32, column_ref.shape, 1)
    vir_own = jnp.sum(jnp.where(spot == group, column_ref[...], 0.0), axis=1, keepdims=True)
    vir_far = row_ref[pl.ds(partner, 1), :]
    occ_far = occ_ref[kpoint_ref[partner, other], slot]
    live_far = slot < count_ref[partner, other]
    far = rows_of(far_refs)
    total = None
    for i in range(occ_slots):
        columns = slice(i * vir_count, (i + 1) * vir_count)
        coulomb = product(own_refs[i][...], far, ((0,), (0,)))
        occ = occ_ref[kpoint_ref[group, block], i] + occ_far
        live = jnp.logical_and(i < count_ref[group, block], live_far)
        scale = jnp.where(live, 1.0, 0.0).astype(jnp.float32)
        amplitude = coulomb * (scale / ((occ - vir_own) - vir_far))
        mixed = (2.0 * amplitude - amplitude.T).astype(jnp.bfloat16)
        if "gamma" in wanted:
            three = product(far, mixed, ((1,), (1,)))
            three = three if not sums else sum_refs[-1][:, columns] + three
            outs[-1][:, columns] = three.astype(outs[-1].dtype)
        if "density" in wanted:
            term = product(mixed, amplitude.astype(jnp.bfloat16), ((1,), (1,)))
            total = term if total is None else total + term
    if "density" not in wanted:
        return
    if sums:
        total = sum_refs[0][...] + total
    if "gamma" in wanted:
        outs[0][...] = total
        return
    total = total * scale_by
    if len(outs) == 2:
        part = vir_count // (wide_count * group_count)
        order = scatter_order(wide_count, group_count)
        total = jnp.concatenate([total[part * place : part * (place + 1)] for place in order], axis=0)
        split_parts(total, scatter_stages(wide_count, group_count)[0], outs[:1], outs[1])
    else:
        outs[0][...] = total


def split_parts(value, bits, sent_refs, kept_ref):
    count = 2 ** len(bits)
    rows = value.shape[0] // count
    places = [lax.axis_index(axis) // mask % 2 for axis, mask in bits]

    def part(flips):
        candidates = [value[place * rows : (place + 1) * rows] for place in range(count)]
        for position, place in enumerate(places):
            upper = place != (flips >> (len(bits) - 1 - position)) % 2
            half = len(candidates) // 2
            candidates = [jnp.where(upper, high, low) for low, high in zip(candidates[:half], candidates[half:])]
        return candidates[0]

    kept_ref[...] = part(0)
    for flips, sent_ref in enumerate(sent_refs, 1):
        sent_ref[...] = part(flips).astype(sent_ref.dtype)


VMEM = pl.BlockSpec(memory_space=pltpu.VMEM)
SMEM = pl.BlockSpec(memory_space=pltpu.SMEM)


def pair_terms(offset, slot, small, own, far, sums, wanted=("density", "gamma"), scale_by=1.0, weight=1):
    aux_count, vir_count = own[0].shape
    width = len(own) * vir_count
    density = jax.ShapeDtypeStruct((vir_count, vir_count), jnp.float32)
    halves = [jax.ShapeDtypeStruct((vir_count // 2, vir_count), kind) for kind in (jnp.bfloat16, jnp.float32)]
    if wanted == ("density",):
        whole = vir_count % (lax.axis_size("wide") * lax.axis_size("narrow")) == 0
        shapes, sums = (halves if whole else [density]), sums[:1]
    elif wanted == ("gamma",):
        shapes, sums = [jax.ShapeDtypeStruct((aux_count, width), jnp.bfloat16)], sums[1:]
    else:
        shapes = [density, jax.ShapeDtypeStruct((aux_count, width), jnp.float32)]
    operands = [*small, *own, *far, *sums]
    flops = weight * (4 * aux_count * width * vir_count + 2 * width * vir_count * vir_count)
    moved = weight * (2 * aux_count * (width + vir_count) + 8 * vir_count * vir_count + 8 * aux_count * width)
    return pl.pallas_call(
        functools.partial(pair_kernel, offset, slot, len(far), len(sums), wanted, scale_by),
        out_shape=tuple(shapes),
        in_specs=[SMEM] * 3 + [VMEM] * (len(operands) - 3),
        out_specs=tuple([VMEM] * len(shapes)),
        compiler_params=pltpu.CompilerParams(vmem_limit_bytes=32 * 1024 * 1024),
        cost_estimate=pl.CostEstimate(flops=flops, bytes_accessed=moved, transcendentals=0),
    )(*operands)


def scatter_stages(wide_count, group_count):
    bits = [("narrow", mask) for mask in reversed(bits_of(group_count))]
    bits += [("wide", mask) for mask in reversed(bits_of(wide_count))]
    stages = [bits[:1]]
    for size in STAGE_BITS:
        stages.append(bits[sum(map(len, stages)) :][:size])
    stages.append(bits[sum(map(len, stages)) :])
    return [stage for stage in stages if stage]


def scatter_order(wide_count, group_count):
    order = [0]
    for axis, mask in reversed([bit for stage in scatter_stages(wide_count, group_count) for bit in stage]):
        step = mask * group_count if axis == "wide" else mask
        order = order + [place + step for place in order]
    return order


def flipped(value, bits, flips):
    group_count = lax.axis_size("narrow")
    masks = [mask * group_count if axis == "wide" else mask for axis, mask in bits]
    step = sum(mask for place, mask in enumerate(reversed(masks)) if flips >> place & 1)
    if len(bits) == 1:
        return flip(value, *bits[0])
    pairs = [(source, source ^ step) for source in range(lax.axis_size("wide") * group_count)]
    return lax.ppermute(value, ("wide", "narrow"), pairs)


def scatter_kernel(bits, got_count, *refs):
    value = refs[got_count][...]
    for got_ref in refs[:got_count]:
        value = value + got_ref[...].astype(jnp.float32)
    outs = refs[got_count + 1 :]
    if bits:
        split_parts(value, bits, outs[:-1], outs[-1])
    elif outs[0].shape == value.shape:
        outs[0][...] = value
    else:
        lanes = outs[0].shape[1]
        tiles = value.shape[1] // lanes
        for tile in range(tiles):
            outs[0][pl.ds(tile, value.shape[0], tiles), :] = value[:, tile * lanes : (tile + 1) * lanes]


def scattered_parts(sent, kept, beside):
    stages = scatter_stages(lax.axis_size("wide"), lax.axis_size("narrow"))
    sents = [sent]
    for position, bits in enumerate(stages):
        rows, columns = kept.shape
        following = stages[position + 1] if position + 1 < len(stages) else []
        if following:
            part = (rows // 2 ** len(following), columns)
            shapes = [jax.ShapeDtypeStruct(part, sent.dtype)] * (2 ** len(following) - 1)
            shapes.append(jax.ShapeDtypeStruct(part, kept.dtype))
        else:
            lanes = 128 if columns % 128 == 0 else columns
            shapes = [jax.ShapeDtypeStruct((rows * columns // lanes, lanes), kept.dtype)]
        got = [flipped(value, bits, flips) for flips, value in enumerate(sents, 1)]
        *sents, kept = pl.pallas_call(
            functools.partial(scatter_kernel, following, len(got)),
            out_shape=tuple(shapes),
            in_specs=[VMEM] * (len(got) + 1),
            out_specs=tuple([VMEM] * len(shapes)),
            compiler_params=pltpu.CompilerParams(vmem_limit_bytes=8 * 1024 * 1024),
            cost_estimate=pl.CostEstimate(flops=rows * columns, bytes_accessed=8 * rows * columns, transcendentals=0),
        )(*got, kept)
        if position == 1:
            sents = [after(value, beside) for value in sents]
    return kept.reshape(-1)


def pack_kernel(slot, sets, raw_ref, *outs):
    block = lax.axis_index("wide")
    for offsets, out_ref in zip(sets, outs):
        for place, offset in enumerate(offsets):
            out_ref[place] = raw_ref[:, jnp.bitwise_xor(block, offset), slot, :]


def packed(raw, slot, sets):
    rows, _, _, vir_count = raw.shape
    return pl.pallas_call(
        functools.partial(pack_kernel, slot, sets),
        out_shape=tuple(jax.ShapeDtypeStruct((len(offsets), rows, vir_count), raw.dtype) for offsets in sets),
        in_specs=[VMEM],
        out_specs=tuple([VMEM] * len(sets)),
        compiler_params=pltpu.CompilerParams(vmem_limit_bytes=32 * 1024 * 1024),
        cost_estimate=pl.CostEstimate(flops=0, bytes_accessed=6 * raw.size, transcendentals=0),
    )(raw)


def sent_direct(raw, slot):
    places = doubled(lax.axis_size("wide"))
    places = places[: len(places) // 2]
    messages = packed(raw, slot, [[place, place ^ 1] for place in places])
    arrived = [flip(message, "wide", place) if place else message for message, place in zip(messages, places)]
    return [jnp.concatenate([message[part] for message in arrived], axis=0) for part in range(2)]


def sent_halving(raw, slot):
    count = lax.axis_size("wide")
    masks = bits_of(count)[-2::-1]
    sets = [[offset for offset in range(count) if offset & masks[0] == sent] for sent in (0, masks[0])]
    kept, message = packed(raw, slot, sets)
    held = {offset: {0: piece} for offset, piece in zip(sets[0], kept)}
    for mask in masks:
        if message is None:
            sent = [held.pop(offset) for offset in sorted(held) if offset & mask]
            message = jnp.stack([piece for pieces in sent for piece in pieces.values()])
        pieces = iter(flip(message, "wide", mask))
        message = None
        for offset in sorted(held):
            held[offset].update({place ^ mask: next(pieces) for place in list(held[offset])})
    order = doubled(count)[: count // 2]
    return [jnp.concatenate([held[part][place] for place in order], axis=0) for part in range(2)]


def after(value, *earlier):
    return lax.optimization_barrier((value, *earlier))[0]


def gathered_rows(raw, metric):
    wide_count, group_count = lax.axis_size("wide"), lax.axis_size("narrow")
    half_turn = [(source, (source + group_count // 2) % group_count) for source in range(group_count)]
    half = metric.shape[1] // 2
    part = lax.dynamic_slice_in_dim(metric, lax.axis_index("narrow") % 2 * half, half, 1)
    steps = []
    for mask in bits_of(wide_count):
        steps.append(flip(part, "wide", mask))
        part = jnp.concatenate([part, steps[-1]], axis=0)
    metric = [part, flip(part, "narrow", 1)]
    rest = []
    for slot in range(raw.shape[2]):
        if slot:
            mine, theirs = sent_halving(after(raw, mine_sent), slot)
            mine, theirs = after(mine, *facing_rows), after(theirs, own_rows[1])
        else:
            mine, theirs = sent_direct(raw, slot)
            mine_sent = steps[0]
        first = lax.ppermute(mine, "narrow", half_turn)
        received = flip(theirs, "wide", 1)
        own_rows = [mine, received]
        facing_rows = [first, lax.ppermute(after(received, *facing) if slot else received, "narrow", half_turn)]
        if slot:
            own += fit(metric, [own_rows], [1])[0]
            rest.append(facing_rows)
        else:
            own, facing = fit(metric, [own_rows, facing_rows], [1, 1])
    return own, facing, metric, rest


def scattered_sum(density):
    wide_count = lax.axis_size("wide")
    group_count = lax.axis_size("narrow")
    wide_bits, narrow_bits = bits_of(wide_count), bits_of(group_count)
    part = density.size // (wide_count * group_count)
    lane = 128 if part % 128 == 0 else part
    value = density.reshape([2] * (len(wide_bits) + len(narrow_bits)) + [part // lane, lane])
    stages = [("narrow", mask, len(wide_bits) + place) for place, mask in enumerate(narrow_bits)]
    stages = stages[::-1] + [("wide", mask, place) for place, mask in reversed(list(enumerate(wide_bits)))]
    for axis, mask, dim in stages:
        bit = (lax.axis_index(axis) // mask) % 2
        sent = lax.dynamic_index_in_dim(value, 1 - bit, dim, keepdims=False).astype(jnp.bfloat16)
        kept = lax.dynamic_index_in_dim(value, bit, dim, keepdims=False)
        value = kept + flip(sent, axis, mask).astype(jnp.float32)
    return value.reshape(-1)


def shards(raw_ints, metric_root, occ_energy, vir_energy, block_kpoint, occ_count):
    _, aux_rows, block_count, occ_slots, vir_count = raw_ints.shape
    wide_count = lax.axis_size("wide")
    group_count = lax.axis_size("narrow")
    my_block = lax.axis_index("wide")
    direct = wide_count <= DIRECT and is_power(wide_count) and wide_count > 2 and group_count % 2 == 0
    small = (occ_energy, block_kpoint, occ_count, vir_energy, vir_energy.T)
    half_turn = [(source, (source + group_count // 2) % group_count) for source in range(group_count)]

    if direct:
        own, facing, metric, rest = gathered_rows(raw_ints[0], metric_root)
    else:
        metric = [lax.all_gather(metric_root, "wide", axis=0, tiled=True)]
        own, rest = [], []
        for slot in range(occ_slots):
            blocks = jnp.transpose(raw_ints[0, :, :, slot, :], (1, 0, 2))
            rows = lax.all_to_all(blocks, "wide", split_axis=0, concat_axis=0, tiled=True)
            rows = rows.reshape(wide_count * aux_rows, vir_count)
            own += fit(metric, [[rows]], [1])[0]
            rest.append([lax.ppermute(rows, "narrow", half_turn)])
        (facing,) = fit(metric, [rest.pop(0)], [1])
    aux_count = own[0].shape[0]

    pair = functools.partial(pair_terms, small=small, own=own)
    ahead, second, first = [facing], [], []
    sums = pair(0, 0, far=facing, sums=(), weight=8)
    for part, *parts in rest:
        last = len(ahead) == occ_slots - 1
        ahead += fit(metric, [[after(part, *sums), *parts]], [LAST_PARTS if last else 1])
    earlier = []
    for slot in range(occ_slots):
        chosen = []
        second.append([])
        first.append([])
        for place, part in enumerate(ahead[slot]):
            part = after(part, *earlier) if place else part
            second[slot].append(from_ahead(part, "wide", 2))
            if wide_count % 2 == 0:
                gate = () if slot and place == 0 else sums
                chosen.append(choice(after(part, *gate), second[slot][-1]))
                first[slot].append(flip(chosen[-1], "wide", 1))
            else:
                first[slot].append(from_ahead(part, "wide", 1))
            if slot and place == 0:
                sums = pair(0, slot, far=ahead[slot], sums=sums)
        earlier = chosen
    for slot in range(occ_slots):
        sums = pair(2, slot, far=second[slot], sums=sums)
    for slot in range(occ_slots - 1):
        sums = pair(1, slot, far=first[slot], sums=sums, weight=3)
    norm_scale = 1.0 / (group_count * wide_count * vir_count)
    last = functools.partial(pair, 1, occ_slots - 1, far=first[-1], sums=sums)
    terms = last(wanted=("density",), scale_by=norm_scale)
    (gamma,) = last(wanted=("gamma",))
    if len(terms) == 2:
        virt_density = scattered_parts(*terms, gamma)
    else:
        virt_density = scattered_sum(*terms)
    return gamma.reshape(1, aux_count, 1, occ_slots, vir_count), virt_density


def solution(mesh):
    placed = (P("narrow", "wide", None, None, None), P("wide", None), P(), P(), P(), P())
    return jax.shard_map(
        shards,
        mesh=mesh,
        in_specs=placed,
        out_specs=(P("narrow", None, "wide", None, None), P(("wide", "narrow"))),
        check_vma=False,
    )
```

```python
import functools

import jax
import jax.numpy as jnp
from jax import lax
from jax.experimental import pallas as pl
from jax.experimental.pallas import tpu as pltpu
from jax.sharding import PartitionSpec as P

WINDOW = 3
DIRECT = 8
STAGE_BITS = (2, 1, 1)
LAST_PARTS = 2


def flip(value, axis, mask):
    pairs = [(source, source ^ mask) for source in range(lax.axis_size(axis))]
    return lax.ppermute(value, axis, pairs)


def from_ahead(value, axis, steps):
    count = lax.axis_size(axis)
    pairs = [(source, (source - steps) % count) for source in range(count)]
    return lax.ppermute(value, axis, pairs)


def is_power(count):
    return count & (count - 1) == 0


def bits_of(count):
    return [1 << bit for bit in reversed(range(count.bit_length() - 1))]


def doubled(count):
    order = [0]
    for mask in bits_of(count):
        order = order + [place ^ mask for place in order]
    return order


def rows_of(refs):
    return refs[0][...] if len(refs) == 1 else jnp.concatenate([ref[...] for ref in refs], axis=0)


def product(left, right, dims):
    return lax.dot_general(left, right, ((dims[0], dims[1]), ((), ())), preferred_element_type=jnp.float32)


def fit_kernel(halves, parts, cuts, *refs):
    metric_refs, refs = refs[:halves], refs[halves:]
    sources, outs = refs[: parts * len(cuts)], refs[parts * len(cuts) :]
    low = lax.axis_index("narrow") % 2 == 0
    for source, cut in enumerate(cuts):
        rows = rows_of(sources[source * parts : (source + 1) * parts])
        fitted = [product(metric_ref[...], rows, ((0,), (0,))) for metric_ref in metric_refs]
        if halves == 2:
            fitted = [jnp.where(low, fitted[0], fitted[1]), jnp.where(low, fitted[1], fitted[0])]
        fitted = jnp.concatenate([part.astype(outs[0].dtype) for part in fitted], axis=0)
        size = fitted.shape[0] // cut
        for place, out_ref in enumerate(outs[:cut]):
            out_ref[...] = fitted[place * size : (place + 1) * size]
        outs = outs[cut:]


def fit(metric, sources, cuts):
    aux_count = sum(half.shape[1] for half in metric)
    vir_count = sources[0][0].shape[1]
    shapes = [
        jax.ShapeDtypeStruct((aux_count // cut, vir_count), sources[0][0].dtype) for cut in cuts for _ in range(cut)
    ]
    operands = [*metric, *[part for source in sources for part in source]]
    flops = 2 * len(sources) * aux_count * aux_count * vir_count
    moved = 2 * aux_count * (aux_count + 2 * len(sources) * vir_count)
    results = pl.pallas_call(
        functools.partial(fit_kernel, len(metric), len(sources[0]), cuts),
        out_shape=tuple(shapes),
        in_specs=[VMEM] * len(operands),
        out_specs=tuple([VMEM] * len(shapes)),
        compiler_params=pltpu.CompilerParams(vmem_limit_bytes=32 * 1024 * 1024),
        cost_estimate=pl.CostEstimate(flops=flops, bytes_accessed=moved, transcendentals=0),
    )(*operands)
    return [list(results[sum(cuts[:place]) : sum(cuts[: place + 1])]) for place in range(len(cuts))]


def choice_kernel(odd_ref, even_ref, out_ref):
    odd = lax.axis_index("wide") % 2 == 1

    @pl.when(odd)
    def _():
        out_ref[...] = odd_ref[...]

    @pl.when(jnp.logical_not(odd))
    def _():
        out_ref[...] = even_ref[...]


def choice(odd, even):
    return pl.pallas_call(
        choice_kernel,
        out_shape=jax.ShapeDtypeStruct(odd.shape, odd.dtype),
        in_specs=[VMEM] * 2,
        out_specs=VMEM,
        compiler_params=pltpu.CompilerParams(vmem_limit_bytes=32 * 1024 * 1024),
        cost_estimate=pl.CostEstimate(flops=0, bytes_accessed=6 * odd.size, transcendentals=0),
    )(odd, even)


def pair_kernel(offset, slot, fars, sums, wanted, scale_by, *refs):
    occ_ref, kpoint_ref, count_ref, row_ref, column_ref = refs[:5]
    occ_slots = occ_ref.shape[1]
    own_refs, refs = refs[5 : 5 + occ_slots], refs[5 + occ_slots :]
    far_refs, refs = refs[:fars], refs[fars:]
    sum_refs, outs = refs[:sums], refs[sums:]
    group_count, wide_count = kpoint_ref.shape
    vir_count = row_ref.shape[1]
    group = lax.axis_index("narrow")
    block = lax.axis_index("wide")
    partner = lax.rem(group + group_count // 2, group_count)
    other = lax.rem(block + offset, wide_count)
    spot = lax.broadcasted_iota(jnp.int32, column_ref.shape, 1)
    vir_own = jnp.sum(jnp.where(spot == group, column_ref[...], 0.0), axis=1, keepdims=True)
    vir_far = row_ref[pl.ds(partner, 1), :]
    occ_far = occ_ref[kpoint_ref[partner, other], slot]
    live_far = slot < count_ref[partner, other]
    far = rows_of(far_refs)
    total = None
    for i in range(occ_slots):
        columns = slice(i * vir_count, (i + 1) * vir_count)
        coulomb = product(own_refs[i][...], far, ((0,), (0,)))
        occ = occ_ref[kpoint_ref[group, block], i] + occ_far
        live = jnp.logical_and(i < count_ref[group, block], live_far)
        scale = jnp.where(live, 1.0, 0.0).astype(jnp.float32)
        amplitude = coulomb * (scale / ((occ - vir_own) - vir_far))
        mixed = (2.0 * amplitude - amplitude.T).astype(jnp.bfloat16)
        if "gamma" in wanted:
            three = product(far, mixed, ((1,), (1,)))
            three = three if not sums else sum_refs[-1][:, columns] + three
            outs[-1][:, columns] = three.astype(outs[-1].dtype)
        if "density" in wanted:
            term = product(mixed, amplitude.astype(jnp.bfloat16), ((1,), (1,)))
            total = term if total is None else total + term
    if "density" not in wanted:
        return
    if sums:
        total = sum_refs[0][...] + total
    if "gamma" in wanted:
        outs[0][...] = total
        return
    total = total * scale_by
    if len(outs) == 2:
        part = vir_count // (wide_count * group_count)
        order = scatter_order(wide_count, group_count)
        total = jnp.concatenate([total[part * place : part * (place + 1)] for place in order], axis=0)
        split_parts(total, scatter_stages(wide_count, group_count)[0], outs[:1], outs[1])
    else:
        outs[0][...] = total


def split_parts(value, bits, sent_refs, kept_ref):
    count = 2 ** len(bits)
    rows = value.shape[0] // count
    places = [lax.axis_index(axis) // mask % 2 for axis, mask in bits]

    def part(flips):
        candidates = [value[place * rows : (place + 1) * rows] for place in range(count)]
        for position, place in enumerate(places):
            upper = place != (flips >> (len(bits) - 1 - position)) % 2
            half = len(candidates) // 2
            candidates = [jnp.where(upper, high, low) for low, high in zip(candidates[:half], candidates[half:])]
        return candidates[0]

    kept_ref[...] = part(0)
    for flips, sent_ref in enumerate(sent_refs, 1):
        sent_ref[...] = part(flips).astype(sent_ref.dtype)


VMEM = pl.BlockSpec(memory_space=pltpu.VMEM)
SMEM = pl.BlockSpec(memory_space=pltpu.SMEM)


def pair_terms(offset, slot, small, own, far, sums, wanted=("density", "gamma"), scale_by=1.0, weight=1):
    aux_count, vir_count = own[0].shape
    width = len(own) * vir_count
    density = jax.ShapeDtypeStruct((vir_count, vir_count), jnp.float32)
    halves = [jax.ShapeDtypeStruct((vir_count // 2, vir_count), kind) for kind in (jnp.bfloat16, jnp.float32)]
    if wanted == ("density",):
        whole = vir_count % (lax.axis_size("wide") * lax.axis_size("narrow")) == 0
        shapes, sums = (halves if whole else [density]), sums[:1]
    elif wanted == ("gamma",):
        shapes, sums = [jax.ShapeDtypeStruct((aux_count, width), jnp.bfloat16)], sums[1:]
    else:
        shapes = [density, jax.ShapeDtypeStruct((aux_count, width), jnp.float32)]
    operands = [*small, *own, *far, *sums]
    flops = weight * (4 * aux_count * width * vir_count + 2 * width * vir_count * vir_count)
    moved = weight * (2 * aux_count * (width + vir_count) + 8 * vir_count * vir_count + 8 * aux_count * width)
    return pl.pallas_call(
        functools.partial(pair_kernel, offset, slot, len(far), len(sums), wanted, scale_by),
        out_shape=tuple(shapes),
        in_specs=[SMEM] * 3 + [VMEM] * (len(operands) - 3),
        out_specs=tuple([VMEM] * len(shapes)),
        compiler_params=pltpu.CompilerParams(vmem_limit_bytes=32 * 1024 * 1024),
        cost_estimate=pl.CostEstimate(flops=flops, bytes_accessed=moved, transcendentals=0),
    )(*operands)


def scatter_stages(wide_count, group_count):
    bits = [("narrow", mask) for mask in reversed(bits_of(group_count))]
    bits += [("wide", mask) for mask in reversed(bits_of(wide_count))]
    stages = [bits[:1]]
    for size in STAGE_BITS:
        stages.append(bits[sum(map(len, stages)) :][:size])
    stages.append(bits[sum(map(len, stages)) :])
    return [stage for stage in stages if stage]


def scatter_order(wide_count, group_count):
    order = [0]
    for axis, mask in reversed([bit for stage in scatter_stages(wide_count, group_count) for bit in stage]):
        step = mask * group_count if axis == "wide" else mask
        order = order + [place + step for place in order]
    return order


def flipped(value, bits, flips):
    group_count = lax.axis_size("narrow")
    masks = [mask * group_count if axis == "wide" else mask for axis, mask in bits]
    step = sum(mask for place, mask in enumerate(reversed(masks)) if flips >> place & 1)
    if len(bits) == 1:
        return flip(value, *bits[0])
    pairs = [(source, source ^ step) for source in range(lax.axis_size("wide") * group_count)]
    return lax.ppermute(value, ("wide", "narrow"), pairs)


def scatter_kernel(bits, got_count, *refs):
    value = refs[got_count][...]
    for got_ref in refs[:got_count]:
        value = value + got_ref[...].astype(jnp.float32)
    outs = refs[got_count + 1 :]
    if bits:
        split_parts(value, bits, outs[:-1], outs[-1])
    elif outs[0].shape == value.shape:
        outs[0][...] = value
    else:
        lanes = outs[0].shape[1]
        tiles = value.shape[1] // lanes
        for tile in range(tiles):
            outs[0][pl.ds(tile, value.shape[0], tiles), :] = value[:, tile * lanes : (tile + 1) * lanes]


def scattered_parts(sent, kept, beside):
    stages = scatter_stages(lax.axis_size("wide"), lax.axis_size("narrow"))
    sents = [sent]
    for position, bits in enumerate(stages):
        rows, columns = kept.shape
        following = stages[position + 1] if position + 1 < len(stages) else []
        if following:
            part = (rows // 2 ** len(following), columns)
            shapes = [jax.ShapeDtypeStruct(part, sent.dtype)] * (2 ** len(following) - 1)
            shapes.append(jax.ShapeDtypeStruct(part, kept.dtype))
        else:
            lanes = 128 if columns % 128 == 0 else columns
            shapes = [jax.ShapeDtypeStruct((rows * columns // lanes, lanes), kept.dtype)]
        got = [flipped(value, bits, flips) for flips, value in enumerate(sents, 1)]
        *sents, kept = pl.pallas_call(
            functools.partial(scatter_kernel, following, len(got)),
            out_shape=tuple(shapes),
            in_specs=[VMEM] * (len(got) + 1),
            out_specs=tuple([VMEM] * len(shapes)),
            compiler_params=pltpu.CompilerParams(vmem_limit_bytes=8 * 1024 * 1024),
            cost_estimate=pl.CostEstimate(flops=rows * columns, bytes_accessed=8 * rows * columns, transcendentals=0),
        )(*got, kept)
        if position == 1:
            sents = [after(value, beside) for value in sents]
    return kept.reshape(-1)


def pack_kernel(slot, sets, raw_ref, *outs):
    block = lax.axis_index("wide")
    for offsets, out_ref in zip(sets, outs):
        for place, offset in enumerate(offsets):
            out_ref[place] = raw_ref[:, jnp.bitwise_xor(block, offset), slot, :]


def packed(raw, slot, sets):
    rows, _, _, vir_count = raw.shape
    return pl.pallas_call(
        functools.partial(pack_kernel, slot, sets),
        out_shape=tuple(jax.ShapeDtypeStruct((len(offsets), rows, vir_count), raw.dtype) for offsets in sets),
        in_specs=[VMEM],
        out_specs=tuple([VMEM] * len(sets)),
        compiler_params=pltpu.CompilerParams(vmem_limit_bytes=32 * 1024 * 1024),
        cost_estimate=pl.CostEstimate(flops=0, bytes_accessed=6 * raw.size, transcendentals=0),
    )(raw)


def sent_direct(raw, slot):
    places = doubled(lax.axis_size("wide"))
    places = places[: len(places) // 2]
    messages = packed(raw, slot, [[place, place ^ 1] for place in places])
    arrived = [flip(message, "wide", place) if place else message for message, place in zip(messages, places)]
    return [jnp.concatenate([message[part] for message in arrived], axis=0) for part in range(2)]


def sent_halving(raw, slot, gates=()):
    count = lax.axis_size("wide")
    masks = bits_of(count)[-2::-1]
    sets = [[offset for offset in range(count) if offset & masks[0] == sent] for sent in (0, masks[0])]
    kept, message = packed(raw, slot, sets)
    held = {offset: {0: piece} for offset, piece in zip(sets[0], kept)}
    for mask in masks:
        if message is None:
            sent = [held.pop(offset) for offset in sorted(held) if offset & mask]
            message = after(jnp.stack([piece for pieces in sent for piece in pieces.values()]), *gates)
        pieces = iter(flip(message, "wide", mask))
        message = None
        for offset in sorted(held):
            held[offset].update({place ^ mask: next(pieces) for place in list(held[offset])})
    order = doubled(count)[: count // 2]
    return [jnp.concatenate([held[part][place] for place in order], axis=0) for part in range(2)]


def after(value, *earlier):
    return lax.optimization_barrier((value, *earlier))[0]


def gathered_rows(raw, metric):
    wide_count, group_count = lax.axis_size("wide"), lax.axis_size("narrow")
    half_turn = [(source, (source + group_count // 2) % group_count) for source in range(group_count)]
    half = metric.shape[1] // 2
    part = lax.dynamic_slice_in_dim(metric, lax.axis_index("narrow") % 2 * half, half, 1)
    steps = []
    for mask in bits_of(wide_count):
        steps.append(flip(part, "wide", mask))
        part = jnp.concatenate([part, steps[-1]], axis=0)
    metric = [part, flip(part, "narrow", 1)]
    rest = []
    for slot in range(raw.shape[2]):
        if slot:
            mine, theirs = sent_halving(after(raw, mine_sent), slot, [received])
            theirs = after(theirs, own_rows[1])
        else:
            mine, theirs = sent_direct(raw, slot)
            mine_sent = steps[0]
        first = lax.ppermute(mine, "narrow", half_turn)
        received = flip(theirs, "wide", 1)
        own_rows = [mine, received]
        facing_rows = [first, lax.ppermute(after(received, *facing) if slot else received, "narrow", half_turn)]
        if slot:
            own += fit(metric, [own_rows], [1])[0]
            rest.append(facing_rows)
        else:
            own, facing = fit(metric, [own_rows, facing_rows], [1, 1])
    return own, facing, metric, rest


def scattered_sum(density):
    wide_count = lax.axis_size("wide")
    group_count = lax.axis_size("narrow")
    wide_bits, narrow_bits = bits_of(wide_count), bits_of(group_count)
    part = density.size // (wide_count * group_count)
    lane = 128 if part % 128 == 0 else part
    value = density.reshape([2] * (len(wide_bits) + len(narrow_bits)) + [part // lane, lane])
    stages = [("narrow", mask, len(wide_bits) + place) for place, mask in enumerate(narrow_bits)]
    stages = stages[::-1] + [("wide", mask, place) for place, mask in reversed(list(enumerate(wide_bits)))]
    for axis, mask, dim in stages:
        bit = (lax.axis_index(axis) // mask) % 2
        sent = lax.dynamic_index_in_dim(value, 1 - bit, dim, keepdims=False).astype(jnp.bfloat16)
        kept = lax.dynamic_index_in_dim(value, bit, dim, keepdims=False)
        value = kept + flip(sent, axis, mask).astype(jnp.float32)
    return value.reshape(-1)


def shards(raw_ints, metric_root, occ_energy, vir_energy, block_kpoint, occ_count):
    _, aux_rows, block_count, occ_slots, vir_count = raw_ints.shape
    wide_count = lax.axis_size("wide")
    group_count = lax.axis_size("narrow")
    my_block = lax.axis_index("wide")
    direct = wide_count <= DIRECT and is_power(wide_count) and wide_count > 2 and group_count % 2 == 0
    small = (occ_energy, block_kpoint, occ_count, vir_energy, vir_energy.T)
    half_turn = [(source, (source + group_count // 2) % group_count) for source in range(group_count)]

    if direct:
        own, facing, metric, rest = gathered_rows(raw_ints[0], metric_root)
    else:
        metric = [lax.all_gather(metric_root, "wide", axis=0, tiled=True)]
        own, rest = [], []
        for slot in range(occ_slots):
            blocks = jnp.transpose(raw_ints[0, :, :, slot, :], (1, 0, 2))
            rows = lax.all_to_all(blocks, "wide", split_axis=0, concat_axis=0, tiled=True)
            rows = rows.reshape(wide_count * aux_rows, vir_count)
            own += fit(metric, [[rows]], [1])[0]
            rest.append([lax.ppermute(rows, "narrow", half_turn)])
        (facing,) = fit(metric, [rest.pop(0)], [1])
    aux_count = own[0].shape[0]

    pair = functools.partial(pair_terms, small=small, own=own)
    ahead, second, first = [facing], [], []
    sums = pair(0, 0, far=facing, sums=(), weight=8)
    for part, *parts in rest:
        last = len(ahead) == occ_slots - 1
        ahead += fit(metric, [[after(part, *sums), *parts]], [LAST_PARTS if last else 1])
    earlier = []
    for slot in range(occ_slots):
        chosen = []
        second.append([])
        first.append([])
        for place, part in enumerate(ahead[slot]):
            part = after(part, *earlier) if place else part
            second[slot].append(from_ahead(part, "wide", 2))
            if wide_count % 2 == 0:
                gate = () if slot and place == 0 else sums
                chosen.append(choice(after(part, *gate), second[slot][-1]))
                first[slot].append(flip(chosen[-1], "wide", 1))
            else:
                first[slot].append(from_ahead(part, "wide", 1))
            if slot and place == 0:
                sums = pair(0, slot, far=ahead[slot], sums=sums)
        earlier = chosen
    for slot in range(occ_slots):
        sums = pair(2, slot, far=second[slot], sums=sums)
    for slot in range(occ_slots - 1):
        sums = pair(1, slot, far=first[slot], sums=sums, weight=3)
    norm_scale = 1.0 / (group_count * wide_count * vir_count)
    last = functools.partial(pair, 1, occ_slots - 1, far=first[-1], sums=sums)
    terms = last(wanted=("density",), scale_by=norm_scale)
    (gamma,) = last(wanted=("gamma",))
    if len(terms) == 2:
        virt_density = scattered_parts(*terms, gamma)
    else:
        virt_density = scattered_sum(*terms)
    return gamma.reshape(1, aux_count, 1, occ_slots, vir_count), virt_density


def solution(mesh):
    placed = (P("narrow", "wide", None, None, None), P("wide", None), P(), P(), P(), P())
    return jax.shard_map(
        shards,
        mesh=mesh,
        in_specs=placed,
        out_specs=(P("narrow", None, "wide", None, None), P(("wide", "narrow"))),
        check_vma=False,
    )
```

```python
import functools

import jax
import jax.numpy as jnp
from jax import lax
from jax.experimental import pallas as pl
from jax.experimental.pallas import tpu as pltpu
from jax.sharding import PartitionSpec as P

WINDOW = 3
DIRECT = 8
STAGE_BITS = (2, 1, 1)
LAST_PARTS = 2


def flip(value, axis, mask):
    pairs = [(source, source ^ mask) for source in range(lax.axis_size(axis))]
    return lax.ppermute(value, axis, pairs)


def from_ahead(value, axis, steps):
    count = lax.axis_size(axis)
    pairs = [(source, (source - steps) % count) for source in range(count)]
    return lax.ppermute(value, axis, pairs)


def is_power(count):
    return count & (count - 1) == 0


def bits_of(count):
    return [1 << bit for bit in reversed(range(count.bit_length() - 1))]


def doubled(count):
    order = [0]
    for mask in bits_of(count):
        order = order + [place ^ mask for place in order]
    return order


def rows_of(refs):
    return refs[0][...] if len(refs) == 1 else jnp.concatenate([ref[...] for ref in refs], axis=0)


def product(left, right, dims):
    return lax.dot_general(left, right, ((dims[0], dims[1]), ((), ())), preferred_element_type=jnp.float32)


def fit_kernel(halves, parts, cuts, *refs):
    metric_refs, refs = refs[:halves], refs[halves:]
    sources, outs = refs[: parts * len(cuts)], refs[parts * len(cuts) :]
    low = lax.axis_index("narrow") % 2 == 0
    for source, cut in enumerate(cuts):
        rows = rows_of(sources[source * parts : (source + 1) * parts])
        fitted = [product(metric_ref[...], rows, ((0,), (0,))) for metric_ref in metric_refs]
        if halves == 2:
            fitted = [jnp.where(low, fitted[0], fitted[1]), jnp.where(low, fitted[1], fitted[0])]
        fitted = jnp.concatenate([part.astype(outs[0].dtype) for part in fitted], axis=0)
        size = fitted.shape[0] // cut
        for place, out_ref in enumerate(outs[:cut]):
            out_ref[...] = fitted[place * size : (place + 1) * size]
        outs = outs[cut:]


def fit(metric, sources, cuts):
    aux_count = sum(half.shape[1] for half in metric)
    vir_count = sources[0][0].shape[1]
    shapes = [
        jax.ShapeDtypeStruct((aux_count // cut, vir_count), sources[0][0].dtype) for cut in cuts for _ in range(cut)
    ]
    operands = [*metric, *[part for source in sources for part in source]]
    flops = 2 * len(sources) * aux_count * aux_count * vir_count
    moved = 2 * aux_count * (aux_count + 2 * len(sources) * vir_count)
    results = pl.pallas_call(
        functools.partial(fit_kernel, len(metric), len(sources[0]), cuts),
        out_shape=tuple(shapes),
        in_specs=[VMEM] * len(operands),
        out_specs=tuple([VMEM] * len(shapes)),
        compiler_params=pltpu.CompilerParams(vmem_limit_bytes=32 * 1024 * 1024),
        cost_estimate=pl.CostEstimate(flops=flops, bytes_accessed=moved, transcendentals=0),
    )(*operands)
    return [list(results[sum(cuts[:place]) : sum(cuts[: place + 1])]) for place in range(len(cuts))]


def choice_kernel(odd_ref, even_ref, out_ref):
    odd = lax.axis_index("wide") % 2 == 1

    @pl.when(odd)
    def _():
        out_ref[...] = odd_ref[...]

    @pl.when(jnp.logical_not(odd))
    def _():
        out_ref[...] = even_ref[...]


def choice(odd, even):
    return pl.pallas_call(
        choice_kernel,
        out_shape=jax.ShapeDtypeStruct(odd.shape, odd.dtype),
        in_specs=[VMEM] * 2,
        out_specs=VMEM,
        compiler_params=pltpu.CompilerParams(vmem_limit_bytes=32 * 1024 * 1024),
        cost_estimate=pl.CostEstimate(flops=0, bytes_accessed=6 * odd.size, transcendentals=0),
    )(odd, even)


def pair_kernel(offset, slot, fars, sums, wanted, scale_by, *refs):
    occ_ref, kpoint_ref, count_ref, row_ref, column_ref = refs[:5]
    occ_slots = occ_ref.shape[1]
    own_refs, refs = refs[5 : 5 + occ_slots], refs[5 + occ_slots :]
    far_refs, refs = refs[:fars], refs[fars:]
    sum_refs, outs = refs[:sums], refs[sums:]
    group_count, wide_count = kpoint_ref.shape
    vir_count = row_ref.shape[1]
    group = lax.axis_index("narrow")
    block = lax.axis_index("wide")
    partner = lax.rem(group + group_count // 2, group_count)
    other = lax.rem(block + offset, wide_count)
    spot = lax.broadcasted_iota(jnp.int32, column_ref.shape, 1)
    vir_own = jnp.sum(jnp.where(spot == group, column_ref[...], 0.0), axis=1, keepdims=True)
    vir_far = row_ref[pl.ds(partner, 1), :]
    occ_far = occ_ref[kpoint_ref[partner, other], slot]
    live_far = slot < count_ref[partner, other]
    far = rows_of(far_refs)
    total = None
    for i in range(occ_slots):
        columns = slice(i * vir_count, (i + 1) * vir_count)
        coulomb = product(own_refs[i][...], far, ((0,), (0,)))
        occ = occ_ref[kpoint_ref[group, block], i] + occ_far
        live = jnp.logical_and(i < count_ref[group, block], live_far)
        scale = jnp.where(live, 1.0, 0.0).astype(jnp.float32)
        amplitude = coulomb * (scale / ((occ - vir_own) - vir_far))
        mixed = (2.0 * amplitude - amplitude.T).astype(jnp.bfloat16)
        if "gamma" in wanted:
            three = product(far, mixed, ((1,), (1,)))
            three = three if not sums else sum_refs[-1][:, columns] + three
            outs[-1][:, columns] = three.astype(outs[-1].dtype)
        if "density" in wanted:
            term = product(mixed, amplitude.astype(jnp.bfloat16), ((1,), (1,)))
            total = term if total is None else total + term
    if "density" not in wanted:
        return
    if sums:
        total = sum_refs[0][...] + total
    if "gamma" in wanted:
        outs[0][...] = total
        return
    total = total * scale_by
    if len(outs) == 2:
        part = vir_count // (wide_count * group_count)
        order = scatter_order(wide_count, group_count)
        total = jnp.concatenate([total[part * place : part * (place + 1)] for place in order], axis=0)
        split_parts(total, scatter_stages(wide_count, group_count)[0], outs[:1], outs[1])
    else:
        outs[0][...] = total


def split_parts(value, bits, sent_refs, kept_ref):
    count = 2 ** len(bits)
    rows = value.shape[0] // count
    places = [lax.axis_index(axis) // mask % 2 for axis, mask in bits]

    def part(flips):
        candidates = [value[place * rows : (place + 1) * rows] for place in range(count)]
        for position, place in enumerate(places):
            upper = place != (flips >> (len(bits) - 1 - position)) % 2
            half = len(candidates) // 2
            candidates = [jnp.where(upper, high, low) for low, high in zip(candidates[:half], candidates[half:])]
        return candidates[0]

    kept_ref[...] = part(0)
    for flips, sent_ref in enumerate(sent_refs, 1):
        sent_ref[...] = part(flips).astype(sent_ref.dtype)


VMEM = pl.BlockSpec(memory_space=pltpu.VMEM)
SMEM = pl.BlockSpec(memory_space=pltpu.SMEM)


def pair_terms(offset, slot, small, own, far, sums, wanted=("density", "gamma"), scale_by=1.0, weight=1):
    aux_count, vir_count = own[0].shape
    width = len(own) * vir_count
    density = jax.ShapeDtypeStruct((vir_count, vir_count), jnp.float32)
    halves = [jax.ShapeDtypeStruct((vir_count // 2, vir_count), kind) for kind in (jnp.bfloat16, jnp.float32)]
    if wanted == ("density",):
        whole = vir_count % (lax.axis_size("wide") * lax.axis_size("narrow")) == 0
        shapes, sums = (halves if whole else [density]), sums[:1]
    elif wanted == ("gamma",):
        shapes, sums = [jax.ShapeDtypeStruct((aux_count, width), jnp.bfloat16)], sums[1:]
    else:
        shapes = [density, jax.ShapeDtypeStruct((aux_count, width), jnp.float32)]
    operands = [*small, *own, *far, *sums]
    flops = weight * (4 * aux_count * width * vir_count + 2 * width * vir_count * vir_count)
    moved = weight * (2 * aux_count * (width + vir_count) + 8 * vir_count * vir_count + 8 * aux_count * width)
    return pl.pallas_call(
        functools.partial(pair_kernel, offset, slot, len(far), len(sums), wanted, scale_by),
        out_shape=tuple(shapes),
        in_specs=[SMEM] * 3 + [VMEM] * (len(operands) - 3),
        out_specs=tuple([VMEM] * len(shapes)),
        compiler_params=pltpu.CompilerParams(vmem_limit_bytes=32 * 1024 * 1024),
        cost_estimate=pl.CostEstimate(flops=flops, bytes_accessed=moved, transcendentals=0),
    )(*operands)


def scatter_stages(wide_count, group_count):
    bits = [("narrow", mask) for mask in reversed(bits_of(group_count))]
    bits += [("wide", mask) for mask in reversed(bits_of(wide_count))]
    stages = [bits[:1]]
    for size in STAGE_BITS:
        stages.append(bits[sum(map(len, stages)) :][:size])
    stages.append(bits[sum(map(len, stages)) :])
    return [stage for stage in stages if stage]


def scatter_order(wide_count, group_count):
    order = [0]
    for axis, mask in reversed([bit for stage in scatter_stages(wide_count, group_count) for bit in stage]):
        step = mask * group_count if axis == "wide" else mask
        order = order + [place + step for place in order]
    return order


def flipped(value, bits, flips):
    group_count = lax.axis_size("narrow")
    masks = [mask * group_count if axis == "wide" else mask for axis, mask in bits]
    step = sum(mask for place, mask in enumerate(reversed(masks)) if flips >> place & 1)
    if len(bits) == 1:
        return flip(value, *bits[0])
    pairs = [(source, source ^ step) for source in range(lax.axis_size("wide") * group_count)]
    return lax.ppermute(value, ("wide", "narrow"), pairs)


def scatter_kernel(bits, got_count, *refs):
    value = refs[got_count][...]
    for got_ref in refs[:got_count]:
        value = value + got_ref[...].astype(jnp.float32)
    outs = refs[got_count + 1 :]
    if bits:
        split_parts(value, bits, outs[:-1], outs[-1])
    elif outs[0].shape == value.shape:
        outs[0][...] = value
    else:
        lanes = outs[0].shape[1]
        tiles = value.shape[1] // lanes
        for tile in range(tiles):
            outs[0][pl.ds(tile, value.shape[0], tiles), :] = value[:, tile * lanes : (tile + 1) * lanes]


def scattered_parts(sent, kept, beside):
    stages = scatter_stages(lax.axis_size("wide"), lax.axis_size("narrow"))
    sents = [sent]
    for position, bits in enumerate(stages):
        rows, columns = kept.shape
        following = stages[position + 1] if position + 1 < len(stages) else []
        if following:
            part = (rows // 2 ** len(following), columns)
            shapes = [jax.ShapeDtypeStruct(part, sent.dtype)] * (2 ** len(following) - 1)
            shapes.append(jax.ShapeDtypeStruct(part, kept.dtype))
        else:
            lanes = 128 if columns % 128 == 0 else columns
            shapes = [jax.ShapeDtypeStruct((rows * columns // lanes, lanes), kept.dtype)]
        got = [flipped(value, bits, flips) for flips, value in enumerate(sents, 1)]
        *sents, kept = pl.pallas_call(
            functools.partial(scatter_kernel, following, len(got)),
            out_shape=tuple(shapes),
            in_specs=[VMEM] * (len(got) + 1),
            out_specs=tuple([VMEM] * len(shapes)),
            compiler_params=pltpu.CompilerParams(vmem_limit_bytes=8 * 1024 * 1024),
            cost_estimate=pl.CostEstimate(flops=rows * columns, bytes_accessed=8 * rows * columns, transcendentals=0),
        )(*got, kept)
        if position == 1:
            sents = [after(value, beside) for value in sents]
    return kept.reshape(-1)


def pack_kernel(slot, sets, raw_ref, *outs):
    block = lax.axis_index("wide")
    for offsets, out_ref in zip(sets, outs):
        for place, offset in enumerate(offsets):
            out_ref[place] = raw_ref[:, jnp.bitwise_xor(block, offset), slot, :]


def packed(raw, slot, sets):
    rows, _, _, vir_count = raw.shape
    return pl.pallas_call(
        functools.partial(pack_kernel, slot, sets),
        out_shape=tuple(jax.ShapeDtypeStruct((len(offsets), rows, vir_count), raw.dtype) for offsets in sets),
        in_specs=[VMEM],
        out_specs=tuple([VMEM] * len(sets)),
        compiler_params=pltpu.CompilerParams(vmem_limit_bytes=32 * 1024 * 1024),
        cost_estimate=pl.CostEstimate(flops=0, bytes_accessed=6 * raw.size, transcendentals=0),
    )(raw)


def sent_direct(raw, slot):
    places = doubled(lax.axis_size("wide"))
    places = places[: len(places) // 2]
    messages = packed(raw, slot, [[place, place ^ 1] for place in places])
    arrived = [flip(message, "wide", place) if place else message for message, place in zip(messages, places)]
    return [jnp.concatenate([message[part] for message in arrived], axis=0) for part in range(2)]


def sent_halving(raw, slot, gates=()):
    count = lax.axis_size("wide")
    masks = bits_of(count)[-2::-1]
    sets = [[offset for offset in range(count) if offset & masks[0] == sent] for sent in (0, masks[0])]
    kept, message = packed(raw, slot, sets)
    held = {offset: {0: piece} for offset, piece in zip(sets[0], kept)}
    for mask in masks:
        if message is None:
            sent = [held.pop(offset) for offset in sorted(held) if offset & mask]
            message = after(jnp.stack([piece for pieces in sent for piece in pieces.values()]), *gates)
        pieces = iter(flip(message, "wide", mask))
        message = None
        for offset in sorted(held):
            held[offset].update({place ^ mask: next(pieces) for place in list(held[offset])})
    order = doubled(count)[: count // 2]
    return [jnp.concatenate([held[part][place] for place in order], axis=0) for part in range(2)]


def after(value, *earlier):
    return lax.optimization_barrier((value, *earlier))[0]


def gathered_rows(raw, metric):
    wide_count, group_count = lax.axis_size("wide"), lax.axis_size("narrow")
    half_turn = [(source, (source + group_count // 2) % group_count) for source in range(group_count)]
    half = metric.shape[1] // 2
    part = lax.dynamic_slice_in_dim(metric, lax.axis_index("narrow") % 2 * half, half, 1)
    steps = []
    for mask in bits_of(wide_count):
        steps.append(flip(part, "wide", mask))
        part = jnp.concatenate([part, steps[-1]], axis=0)
    metric = [part, flip(part, "narrow", 1)]
    rest = []
    for slot in range(raw.shape[2]):
        if slot:
            mine, theirs = sent_halving(after(raw, mine_sent), slot, [received])
        else:
            mine, theirs = sent_direct(raw, slot)
            mine_sent = steps[0]
        first = lax.ppermute(mine, "narrow", half_turn)
        received = flip(theirs, "wide", 1)
        own_rows = [mine, received]
        facing_rows = [first, lax.ppermute(after(received, *facing) if slot else received, "narrow", half_turn)]
        if slot:
            own += fit(metric, [own_rows], [1])[0]
            rest.append(facing_rows)
        else:
            own, facing = fit(metric, [own_rows, facing_rows], [1, 1])
    return own, facing, metric, rest


def scattered_sum(density):
    wide_count = lax.axis_size("wide")
    group_count = lax.axis_size("narrow")
    wide_bits, narrow_bits = bits_of(wide_count), bits_of(group_count)
    part = density.size // (wide_count * group_count)
    lane = 128 if part % 128 == 0 else part
    value = density.reshape([2] * (len(wide_bits) + len(narrow_bits)) + [part // lane, lane])
    stages = [("narrow", mask, len(wide_bits) + place) for place, mask in enumerate(narrow_bits)]
    stages = stages[::-1] + [("wide", mask, place) for place, mask in reversed(list(enumerate(wide_bits)))]
    for axis, mask, dim in stages:
        bit = (lax.axis_index(axis) // mask) % 2
        sent = lax.dynamic_index_in_dim(value, 1 - bit, dim, keepdims=False).astype(jnp.bfloat16)
        kept = lax.dynamic_index_in_dim(value, bit, dim, keepdims=False)
        value = kept + flip(sent, axis, mask).astype(jnp.float32)
    return value.reshape(-1)


def shards(raw_ints, metric_root, occ_energy, vir_energy, block_kpoint, occ_count):
    _, aux_rows, block_count, occ_slots, vir_count = raw_ints.shape
    wide_count = lax.axis_size("wide")
    group_count = lax.axis_size("narrow")
    my_block = lax.axis_index("wide")
    direct = wide_count <= DIRECT and is_power(wide_count) and wide_count > 2 and group_count % 2 == 0
    small = (occ_energy, block_kpoint, occ_count, vir_energy, vir_energy.T)
    half_turn = [(source, (source + group_count // 2) % group_count) for source in range(group_count)]

    if direct:
        own, facing, metric, rest = gathered_rows(raw_ints[0], metric_root)
    else:
        metric = [lax.all_gather(metric_root, "wide", axis=0, tiled=True)]
        own, rest = [], []
        for slot in range(occ_slots):
            blocks = jnp.transpose(raw_ints[0, :, :, slot, :], (1, 0, 2))
            rows = lax.all_to_all(blocks, "wide", split_axis=0, concat_axis=0, tiled=True)
            rows = rows.reshape(wide_count * aux_rows, vir_count)
            own += fit(metric, [[rows]], [1])[0]
            rest.append([lax.ppermute(rows, "narrow", half_turn)])
        (facing,) = fit(metric, [rest.pop(0)], [1])
    aux_count = own[0].shape[0]

    pair = functools.partial(pair_terms, small=small, own=own)
    ahead, second, first = [facing], [], []
    sums = pair(0, 0, far=facing, sums=(), weight=8)
    for part, *parts in rest:
        last = len(ahead) == occ_slots - 1
        ahead += fit(metric, [[after(part, *sums), *parts]], [LAST_PARTS if last else 1])
    earlier = []
    for slot in range(occ_slots):
        chosen = []
        second.append([])
        first.append([])
        for place, part in enumerate(ahead[slot]):
            part = after(part, *earlier) if place else part
            second[slot].append(from_ahead(part, "wide", 2))
            if wide_count % 2 == 0:
                gate = () if slot and place == 0 else sums
                chosen.append(choice(after(part, *gate), second[slot][-1]))
                first[slot].append(flip(chosen[-1], "wide", 1))
            else:
                first[slot].append(from_ahead(part, "wide", 1))
            if slot and place == 0:
                sums = pair(0, slot, far=ahead[slot], sums=sums)
        earlier = chosen
    for slot in range(occ_slots):
        sums = pair(2, slot, far=second[slot], sums=sums)
    for slot in range(occ_slots - 1):
        sums = pair(1, slot, far=first[slot], sums=sums, weight=3)
    norm_scale = 1.0 / (group_count * wide_count * vir_count)
    last = functools.partial(pair, 1, occ_slots - 1, far=first[-1], sums=sums)
    terms = last(wanted=("density",), scale_by=norm_scale)
    (gamma,) = last(wanted=("gamma",))
    if len(terms) == 2:
        virt_density = scattered_parts(*terms, gamma)
    else:
        virt_density = scattered_sum(*terms)
    return gamma.reshape(1, aux_count, 1, occ_slots, vir_count), virt_density


def solution(mesh):
    placed = (P("narrow", "wide", None, None, None), P("wide", None), P(), P(), P(), P())
    return jax.shard_map(
        shards,
        mesh=mesh,
        in_specs=placed,
        out_specs=(P("narrow", None, "wide", None, None), P(("wide", "narrow"))),
        check_vma=False,
    )
```
